256 devices in a mesh: group: 4 (over y), psg: 64 (over x, z, core).
Axes of the slice: x: 4, y: 4, z: 8, core: 2. Of those that a mesh axis runs over, the one named last changes fastest.
Arguments:
- queries: bfloat16 [4096, 2048], P(('group', 'psg')), parts along dimension 0, as said below
- keys: bfloat16 [256, 512, 2048], P(('group', 'psg')), parts along dimension 0
- values: bfloat16 [256, 512, 2048], P(('group', 'psg')), parts along dimension 0, may hold values from -6 to 6
- grad_out: bfloat16 [4096, 2048], P(('group', 'psg')), parts along dimension 0, may hold values from -6 to 6
- lengths: int32 [256], P(('group', 'psg')), parts along dimension 0, may hold values from 1 to 8, 256 in all
- slot_query: int32 [256], P(('group', 'psg')), parts along dimension 0, may hold values from 0 to 1, as said below
Outputs:
- grad_queries: bfloat16 [4096, 2048], P(('group', 'psg')), parts along dimension 0
- grad_keys: bfloat16 [256, 512, 2048], P(('group', 'psg')), parts along dimension 0
- grad_values: bfloat16 [256, 512, 2048], P(('group', 'psg')), parts along dimension 0
The draws below stay inside these ranges and needn't reach their ends.
There are 4 independent parts, one for each index of `group`. The reference program is written for one: setup_inputs(seed, part) draws one part's arguments, and reference() takes and returns one part's arrays. A program takes and returns all parts, laid end to end along the dimension named above; each array names one. Nothing has to cross between parts.
Inputs may be any that keep to these rules, and one draw needn't show every extreme that they name: `slot_query`: every query 0 to 1 owns exactly 32 passages. `queries`: some query rows may align with keys, so that scores can reach a few hundred.
All inputs are finite; a program needn't handle non-finite values. No bound on the sum of `lengths` on one device may be relied on, other than what follows from the above.
Results may differ from the reference program's by a relative error of at most 0.0051.
Values may be sent and summed in bfloat16 or wider, within the bound.
No kernel may reach another device: no remote copies, remote signals or barrier semaphores. Data moves between devices by JAX's collectives and lax.ppermute only.
A program may use at most 256 MiB of HBM per device.

```python
import math
import jax
import jax.numpy as jnp
import numpy as np
from jax import lax

HEADS = 32
HDIM = 64
BKT = 64
MAXB = 8
BKT_DEV = 4
QRY = 2
DEC = 512
PASSAGES = 64
PSG_Q = 32
LMAX = 512
HD = 2048
ROWS = 1024
N_PSG = 64


def shared_order(key):
    return jax.random.permutation(jax.random.fold_in(key, 101), PASSAGES)


def base_keys(key):
    return 0.35 * jax.random.normal(jax.random.fold_in(key, 102), (PASSAGES, LMAX, HD), jnp.float32)


def draw_slot_query(key, part):
    order = shared_order(key)
    return (order // PSG_Q).astype(jnp.int32)


def draw_keys(key, part):
    base = base_keys(key)
    return base.astype(jnp.bfloat16)


def draw_queries(key, part):
    key = jax.random.fold_in(key, 3)
    drawn = 0.35 * jax.random.normal(key, (QRY, DEC, HD), jnp.float32)
    return drawn.reshape(QRY * DEC, HD).astype(jnp.bfloat16)


def shard_levels(own_key, dims, cuts, least, top_value):
    factor_of = 1.0
    for dim, blocks in cuts:
        heights = jax.random.uniform(jax.random.fold_in(jax.random.fold_in(own_key, 6), dim), (blocks,), jnp.float32, least / len(cuts), top_value / len(cuts))
        factor_of = factor_of * jnp.repeat(jnp.exp(heights), dims[dim] // blocks).reshape((-1,) + (1,) * (len(dims) - 1 - dim))
    return factor_of


def split_up(number_of, total, reach, skew):
    loads = [(1 << 20) // math.isqrt(standing ** skew) + 1 for standing in range(2, number_of + 1)]
    surplus, counts = total - reach - (number_of - 1), [1] * (number_of - 1)
    while surplus > 0:
        candidates = [i for i in range(number_of - 1) if counts[i] < reach]
        pool, budget = sum([loads[i] for i in candidates]), surplus
        for i in candidates:
            addition = min(reach - counts[i], max(1, budget * loads[i] // pool), surplus)
            counts[i] = counts[i] + addition
            surplus = surplus - addition
    return np.array([reach] + counts)


def uneven_parts(stream_key, count, total, most, lean):
    if count == 2:
        one = jax.random.randint(stream_key, (), max(1, total - most), min(most, total - 1) + 1)
        return jnp.stack([one, total - one])
    sizes = jnp.asarray(split_up(count, total, most, lean), jnp.int32)
    twos = (count - 1) // 2
    giver, taker = sizes[1:1 + 2 * twos:2], sizes[2:2 + 2 * twos:2]
    margin = jnp.minimum(giver - 1, most - taker)
    passed = jax.random.randint(jax.random.fold_in(stream_key, 1), (twos,), 0, 1 << 20) % (margin + 1)
    sizes = sizes.at[1:1 + 2 * twos:2].set(giver - passed).at[2:2 + 2 * twos:2].set(taker + passed)
    return sizes[jax.random.permutation(jax.random.fold_in(stream_key, 2), count)]


def bell_draw(rng, dims, width, reach, split=(), kind=jnp.bfloat16):
    values = width * jax.random.normal(rng, dims, jnp.float32)
    if split:
        values = values * shard_levels(rng, dims, split, -0.22, 0.18)
    return jnp.clip(values, -reach, reach).astype(kind)


def setup_inputs(seed: int = 0, part: int = 0) -> dict:
    key_list = jax.random.split(jax.random.key(seed), 7)
    part_splits = jax.random.split(jax.random.fold_in(key_list[6], part), 7)
    return {
        "queries": draw_queries(jax.random.fold_in(jax.random.fold_in(key_list[6], part), 71), part),
        "keys": draw_keys(jax.random.fold_in(jax.random.fold_in(key_list[6], part), 71), part),
        "values": bell_draw(part_splits[2], (PASSAGES, LMAX, HD), 1.0, 6.0, ((0, 64),)),
        "grad_out": bell_draw(part_splits[3], (ROWS, HD), 1.0, 6.0, ((0, 64),)),
        "lengths": uneven_parts(part_splits[4], PASSAGES, BKT_DEV * N_PSG, MAXB, 2).astype(jnp.int32),
        "slot_query": draw_slot_query(jax.random.fold_in(jax.random.fold_in(key_list[6], part), 71), part),
    }


def passage_scores(q_rows, g_rows, key_block, val_block, count):
    q_heads = q_rows.astype(jnp.float32).reshape(DEC, HEADS, HDIM)
    g_heads = g_rows.astype(jnp.float32).reshape(DEC, HEADS, HDIM)
    k_heads = key_block.astype(jnp.float32).reshape(LMAX, HEADS, HDIM)
    v_heads = val_block.astype(jnp.float32).reshape(LMAX, HEADS, HDIM)
    scores = jnp.einsum('rhd,khd->hrk', q_heads, k_heads)
    is_valid = jnp.arange(LMAX) < count * BKT
    scores = jnp.where(is_valid[None, None, :], scores, -jnp.inf)
    upstream = jnp.einsum('rhd,khd->hrk', g_heads, v_heads)
    return scores, upstream, q_heads, g_heads, k_heads


def reference(queries, keys, values, grad_out, lengths, slot_query):
    grouped_q = queries.reshape(QRY, DEC, HD)
    grouped_g = grad_out.reshape(QRY, DEC, HD)

    def first_pass(passage_items):
        key_block, val_block, count, owner = passage_items
        scores, upstream, _, _, _ = passage_scores(grouped_q[owner], grouped_g[owner], key_block, val_block, count)
        local_max = jnp.max(scores, axis=-1)
        weights = jnp.exp(scores - local_max[..., None])
        return local_max, jnp.sum(weights, axis=-1), jnp.sum(weights * upstream, axis=-1)

    local_max, local_sum, local_dot = lax.map(first_pass, (keys, values, lengths, slot_query))
    member = slot_query[:, None] == jnp.arange(QRY, dtype=jnp.int32)[None, :]
    row_top = jnp.max(jnp.where(member[:, :, None, None], local_max[:, None], -jnp.inf), axis=0)
    factor = jnp.exp(local_max - row_top[slot_query])
    weight = member.astype(jnp.float32)
    row_total = jnp.einsum('pq,phr->qhr', weight, local_sum * factor)
    dotted = jnp.einsum('pq,phr->qhr', weight, local_dot * factor)
    row_delta = dotted / row_total

    def second_pass(passage_items):
        key_block, val_block, count, owner = passage_items
        scores, upstream, q_heads, g_heads, k_heads = passage_scores(grouped_q[owner], grouped_g[owner], key_block, val_block, count)
        attn_probs = jnp.exp(scores - row_top[owner][..., None]) / row_total[owner][..., None]
        probs_low = attn_probs.astype(jnp.bfloat16)
        dscore = (attn_probs * (upstream - row_delta[owner][..., None])).astype(jnp.bfloat16)
        grad_val = jnp.einsum('hrk,rhd->khd', probs_low.astype(jnp.float32), g_heads).astype(jnp.bfloat16)
        grad_key = jnp.einsum('hrk,rhd->khd', dscore.astype(jnp.float32), q_heads).astype(jnp.bfloat16)
        dq_term = jnp.einsum('hrk,khd->rhd', dscore.astype(jnp.float32), k_heads)
        return grad_key.reshape(LMAX, HD), grad_val.reshape(LMAX, HD), dq_term.reshape(DEC, HD)

    grad_keys, grad_values, dq_terms = lax.map(second_pass, (keys, values, lengths, slot_query))
    grad_queries = jnp.einsum('pq,prd->qrd', weight, dq_terms).reshape(ROWS, HD).astype(jnp.bfloat16)
    return grad_queries, grad_keys, grad_values
```

```python
import jax
import jax.numpy as jnp
from jax import lax
from jax.experimental import pallas as pl
from jax.experimental.pallas import tpu as pltpu
from jax.sharding import Mesh
from jax.sharding import PartitionSpec as P

HDIM = 64
BKT = 64
QRY = 2
LANES = 128
F32 = jnp.float32
BF16 = jnp.bfloat16
CHIP = ("x", "z")


def shifted(value, axis, size, step):
    return lax.ppermute(value, axis, [(i, (i + step) % size) for i in range(size)])


def swap_cores(value):
    return lax.ppermute(value, "core", [(0, 1), (1, 0)])


def placed(pieces, index, count):
    whole = jnp.zeros((count,) + pieces[0][1].shape, pieces[0][1].dtype)
    for offset, piece in pieces:
        whole = lax.dynamic_update_slice_in_dim(whole, piece[None], (index + offset) % count, 0)
    return whole


def direct_gather(value, axis, size):
    pieces = [(0, value)]
    for step in range(1, size):
        pieces.append((-step, shifted(value, axis, size, step)))
    return placed(pieces, lax.axis_index(axis), size)


def ring_gather(value, axis, size):
    pieces, up, down = [(0, value)], value, value
    for step in range(1, size // 2):
        up, down = shifted(up, axis, size, 1), shifted(down, axis, size, -1)
        pieces += [(-step, up), (step, down)]
    half = value.shape[0] // 2
    last = jnp.concatenate(
        [shifted(up[:half], axis, size, 1), shifted(down[half:], axis, size, -1)], 0
    )
    pieces.append((size // 2, last))
    return placed(pieces, lax.axis_index(axis), size)


def gather_rows(value, x_size, z_size, x_first):
    rows, width = value.shape
    if x_first:
        part = direct_gather(value, "x", x_size).reshape(x_size * rows, width)
        whole = ring_gather(part, "z", z_size).reshape(z_size, x_size, rows, width)
        return whole.transpose(1, 0, 2, 3).reshape(-1, width)
    part = direct_gather(value, "z", z_size).reshape(z_size * rows, width)
    return ring_gather(part, "x", x_size).reshape(-1, width)


def dot_nt(a, b):
    return lax.dot_general(a, b, (((1,), (1,)), ((), ())), preferred_element_type=F32)


def dot_nn(a, b):
    return lax.dot_general(a, b, (((1,), (0,)), ((), ())), preferred_element_type=F32)


def over_chunks(buckets, step):
    fours = buckets // 4

    def body(i, carry):
        step(pl.multiple_of(i * (4 * BKT), 4 * BKT), 4 * BKT)
        return carry

    lax.fori_loop(0, fours, body, 0)
    start = fours * (4 * BKT)

    @pl.when((buckets & 2) != 0)
    def _():
        step(pl.multiple_of(start, 4 * BKT), 2 * BKT)

    @pl.when((buckets & 1) != 0)
    def _():
        step(pl.multiple_of(start + (buckets & 2) * BKT, BKT), BKT)


def load_keys(own_k, sib_k, own_v, sib_v, keys, vals):
    keys[0], keys[1] = own_k[...], sib_k[...]
    vals[0], vals[1] = own_v[...], sib_v[...]


def load_rows(owner, rows, q_ref, g_ref, q_head, g_head):
    at = pl.ds(pl.multiple_of(owner * rows, rows), rows)
    q_rows, g_rows = q_ref[at, :], g_ref[at, :]
    lane = lax.broadcasted_iota(jnp.int32, (rows, LANES), 1)
    for h in range(2):
        mine = (lane < HDIM) if h == 0 else (lane >= HDIM)
        q_head[h] = jnp.where(mine, q_rows, jnp.zeros_like(q_rows))
        g_head[h] = jnp.where(mine, g_rows, jnp.zeros_like(g_rows))


def stats_kernel(info, own_k, sib_k, own_v, sib_v, q_ref, g_ref, out_ref,
                 keys, vals, q_head, g_head, top, total, dotted):
    rows = q_head.shape[1]
    load_keys(own_k, sib_k, own_v, sib_v, keys, vals)

    def passage(p, carry):
        load_rows(info[1 + p], rows, q_ref, g_ref, q_head, g_head)
        top[...] = jnp.full(top.shape, -jnp.inf, F32)
        total[...] = jnp.zeros(total.shape, F32)
        dotted[...] = jnp.zeros(dotted.shape, F32)

        def step(start, count):
            k_part = keys[p, pl.ds(start, count), :]
            v_part = vals[p, pl.ds(start, count), :]
            for h in range(2):
                scores = dot_nt(k_part, q_head[h]).reshape(count // 8, 8, rows)
                upstream = dot_nt(v_part, g_head[h]).reshape(count // 8, 8, rows)
                old = top[h]
                new = jnp.maximum(old, jnp.max(scores, axis=0))
                weights = jnp.exp(scores - new[None])
                factor = jnp.exp(old - new)
                top[h] = new
                total[h] = total[h] * factor + jnp.sum(weights, axis=0)
                dotted[h] = dotted[h] * factor + jnp.sum(weights * upstream, axis=0)

        over_chunks(info[3 + p], step)
        half = rows // 2
        for h in range(2):
            peak = jnp.max(top[h], axis=0, keepdims=True)
            factor = jnp.exp(top[h] - peak)
            stats = (
                peak,
                jnp.sum(total[h] * factor, axis=0, keepdims=True),
                jnp.sum(dotted[h] * factor, axis=0, keepdims=True),
                jnp.full((1, rows), info[1 + p].astype(F32)),
            )
            for s in range(2):
                for t, stat in enumerate(stats):
                    out_ref[2 * h + s, pl.ds(2 * t + p, 1), :] = stat[:, s * half:(s + 1) * half]
        return carry

    lax.fori_loop(0, 2, passage, 0)


def merge_kernel(in_ref, out_ref):
    chips = in_ref.shape[0]
    merged = []
    tops = [in_ref[:, t, :] for t in range(2)]
    sums = [in_ref[:, 2 + t, :] for t in range(2)]
    dots = [in_ref[:, 4 + t, :] for t in range(2)]
    owners = [in_ref[:, 6 + t, :] for t in range(2)]
    for query in range(QRY):
        held = [jnp.where(owners[t] == query, tops[t], -jnp.inf) for t in range(2)]
        peak = jnp.max(jnp.maximum(held[0], held[1]), axis=0, keepdims=True)
        factors = [jnp.exp(held[t] - peak) for t in range(2)]
        total = jnp.sum(sums[0] * factors[0] + sums[1] * factors[1], axis=0, keepdims=True)
        dotted = jnp.sum(dots[0] * factors[0] + dots[1] * factors[1], axis=0, keepdims=True)
        merged.append((peak + jnp.log(total), dotted / total))
    table = jnp.concatenate(
        [merged[0][0], merged[1][0], merged[0][1], merged[1][1]]
        + [jnp.zeros_like(merged[0][0])] * 4, axis=0
    )
    out_ref[...] = jnp.broadcast_to(table[None], out_ref.shape)


def grads_kernel(info, own_k, sib_k, own_v, sib_v, q_ref, g_ref, st_ref,
                 own_dk, sib_dk, own_dv, sib_dv, dq_ref,
                 keys, vals, q_head, g_head, dkeys, dvals, turned, dq_sum):
    rows = q_head.shape[1]
    load_keys(own_k, sib_k, own_v, sib_v, keys, vals)
    dkeys[...] = jnp.zeros(dkeys.shape, BF16)
    dvals[...] = jnp.zeros(dvals.shape, BF16)
    dq_sum[...] = jnp.zeros(dq_sum.shape, F32)

    def passage(p, carry):
        owner = info[1 + p]
        load_rows(owner, rows, q_ref, g_ref, q_head, g_head)
        turned[...] = jnp.zeros(turned.shape, F32)

        def row_stat(h, t):
            return jnp.concatenate(
                [st_ref[2 * h + s, pl.ds(2 * t + owner, 1), :] for s in range(2)], axis=1
            )

        def step(start, count):
            at = pl.ds(start, count)
            k_part, v_part = keys[p, at, :], vals[p, at, :]
            k_turned = k_part.T
            dk_part = dv_part = None
            for h in range(2):
                probs = jnp.exp(dot_nt(k_part, q_head[h]) - row_stat(h, 0))
                dscore = (probs * (dot_nt(v_part, g_head[h]) - row_stat(h, 1))).astype(BF16)
                dv_term = dot_nn(probs.astype(BF16), g_head[h])
                dk_term = dot_nn(dscore, q_head[h])
                dv_part = dv_term if h == 0 else dv_part + dv_term
                dk_part = dk_term if h == 0 else dk_part + dk_term
                own = slice(h * HDIM, (h + 1) * HDIM)
                turned[own, :] += dot_nn(k_turned[own, :], dscore)
            dkeys[p, at, :] = dk_part.astype(BF16)
            dvals[p, at, :] = dv_part.astype(BF16)

        over_chunks(info[3 + p], step)
        at = pl.ds(pl.multiple_of(owner * rows, rows), rows)
        dq_sum[at, :] += turned[...].T
        return carry

    lax.fori_loop(0, 2, passage, 0)
    own_dk[...], sib_dk[...] = dkeys[0], dkeys[1]
    own_dv[...], sib_dv[...] = dvals[0], dvals[1]
    dq_ref[...] = dq_sum[...].astype(BF16)


def per_device(x_size, z_size, queries, keys, values, grad_out, lengths, slot_query):
    chips = x_size * z_size
    core = lax.axis_index("core")
    slots, width = keys.shape[1], keys.shape[2]
    half = width // 2
    pairs = half // LANES
    keys, values = keys[0], values[0]

    mine = jnp.concatenate([slot_query, lengths])
    theirs = swap_cores(mine)
    info = jnp.stack([core, mine[0], theirs[0], mine[1], theirs[1]]).astype(jnp.int32)

    def features(value, of_core):
        return lax.dynamic_slice_in_dim(value, of_core * half, half, value.ndim - 1)

    def chip_rows(value):
        return features(lax.all_gather(value, "core", axis=0, tiled=True), core)

    whole_q = gather_rows(chip_rows(queries), x_size, z_size, True)
    whole_g = gather_rows(chip_rows(grad_out), x_size, z_size, False)
    sib_k = swap_cores(features(keys, 1 - core))
    sib_v = swap_cores(features(values, 1 - core))
    all_rows = whole_q.shape[0]
    rows = all_rows // QRY
    limit = pltpu.CompilerParams(
        dimension_semantics=("arbitrary",), vmem_limit_bytes=48 * 1024 * 1024
    )

    own_block = pl.BlockSpec((slots, LANES), lambda i, info: (0, info[0] * pairs + i))
    sib_block = pl.BlockSpec((slots, LANES), lambda i, info: (0, i))
    row_block = pl.BlockSpec((all_rows, LANES), lambda i, info: (0, i))
    stat_block = pl.BlockSpec((4, 8, rows // 2), lambda i, info: (i, 0, 0))
    stat_shape = jax.ShapeDtypeStruct((4 * pairs, 8, rows // 2), F32)
    key_scratch = [pltpu.VMEM((2, slots, LANES), BF16)] * 2
    row_scratch = [pltpu.VMEM((2, rows, LANES), BF16)] * 2
    operands = (info, keys, sib_k, values, sib_v, whole_q, whole_g)
    in_blocks = [own_block, sib_block, own_block, sib_block, row_block, row_block]

    stats = pl.pallas_call(
        stats_kernel,
        grid_spec=pltpu.PrefetchScalarGridSpec(
            num_scalar_prefetch=1,
            grid=(pairs,),
            in_specs=in_blocks,
            out_specs=stat_block,
            scratch_shapes=key_scratch + row_scratch + [pltpu.VMEM((2, 8, rows), F32)] * 3,
        ),
        out_shape=stat_shape,
        compiler_params=limit,
        name="row_stats",
    )(*operands)

    stats = lax.all_to_all(stats, CHIP, 0, 0, tiled=True)
    stats = pl.pallas_call(
        merge_kernel,
        out_shape=stat_shape,
        in_specs=[pl.BlockSpec(memory_space=pltpu.VMEM)],
        out_specs=pl.BlockSpec(memory_space=pltpu.VMEM),
        name="merge_stats",
    )(stats)
    stats = lax.all_to_all(stats, CHIP, 0, 0, tiled=True)

    own_dk, sib_dk, own_dv, sib_dv, dq = pl.pallas_call(
        grads_kernel,
        grid_spec=pltpu.PrefetchScalarGridSpec(
            num_scalar_prefetch=1,
            grid=(pairs,),
            in_specs=in_blocks + [stat_block],
            out_specs=[own_block, sib_block, own_block, sib_block, row_block],
            scratch_shapes=key_scratch + row_scratch + key_scratch
            + [pltpu.VMEM((LANES, rows), F32), pltpu.VMEM((all_rows, LANES), F32)],
        ),
        out_shape=[
            jax.ShapeDtypeStruct((slots, width), BF16),
            jax.ShapeDtypeStruct((slots, half), BF16),
            jax.ShapeDtypeStruct((slots, width), BF16),
            jax.ShapeDtypeStruct((slots, half), BF16),
            jax.ShapeDtypeStruct((all_rows, half), BF16),
        ],
        compiler_params=limit,
        name="gradients",
    )(*operands, stats)

    chip_rows_count = all_rows // chips
    terms = lax.all_to_all(dq.reshape(chips, chip_rows_count, half), CHIP, 0, 0, tiled=True)
    summed = jnp.sum(terms.astype(F32), axis=0).astype(BF16)
    own_rows = chip_rows_count // 2
    kept = lax.dynamic_slice_in_dim(summed, core * own_rows, own_rows, 0)
    given = swap_cores(lax.dynamic_slice_in_dim(summed, (1 - core) * own_rows, own_rows, 0))
    grad_queries = jnp.where(
        core == 0, jnp.concatenate([kept, given], 1), jnp.concatenate([given, kept], 1)
    )

    def completed(own, sib):
        return lax.dynamic_update_slice_in_dim(own, swap_cores(sib), (1 - core) * half, 1)[None]

    return grad_queries, completed(own_dk, sib_dk), completed(own_dv, sib_dv)


def solution(mesh):
    groups = mesh.devices.shape[0]
    x_size, z_size = 4, 8
    fine = Mesh(
        mesh.devices.reshape(groups, x_size, z_size, 2), ("group", "x", "z", "core")
    )
    at = ("group", "x", "z", "core")

    def step(*args):
        return per_device(x_size, z_size, *args)

    return jax.shard_map(
        step,
        mesh=fine,
        in_specs=(P(at, None), P(at, None, None), P(at, None, None), P(at, None), P(at), P(at)),
        out_specs=(P(at, None), P(at, None, None), P(at, None, None)),
        check_vma=False,
    )
```

```python
import functools

import jax
import jax.numpy as jnp
from jax import lax
from jax.experimental import pallas as pl
from jax.experimental.pallas import tpu as pltpu
from jax.sharding import Mesh
from jax.sharding import PartitionSpec as P

HDIM = 64
BKT = 64
QRY = 2
LANES = 128
F32 = jnp.float32
BF16 = jnp.bfloat16
CHIP = ("x", "z")


def swap_cores(value):
    return lax.ppermute(value, "core", [(0, 1), (1, 0)])


def repeated(value, count):
    return jnp.broadcast_to(value[None], (count,) + value.shape)


def gather_x_then_z(value, x_size):
    columns = lax.all_to_all(repeated(value, x_size), "x", 0, 0, tiled=True)
    return lax.all_gather(columns, "z", axis=0, tiled=False)


def gather_z_then_x(value, x_size, z_size):
    column = lax.all_to_all(repeated(value, z_size), "z", 0, 0, tiled=True)
    return lax.all_to_all(repeated(column, x_size), "x", 0, 0, tiled=True)


def dot_nt(a, b):
    return lax.dot_general(a, b, (((1,), (1,)), ((), ())), preferred_element_type=F32)


def dot_nn(a, b):
    return lax.dot_general(a, b, (((1,), (0,)), ((), ())), preferred_element_type=F32)


def over_chunks(buckets, step):
    fours = buckets // 4

    def body(i, carry):
        step(pl.multiple_of(i * (4 * BKT), 4 * BKT), 4 * BKT)
        return carry

    lax.fori_loop(0, fours, body, 0)
    start = fours * (4 * BKT)

    @pl.when((buckets & 2) != 0)
    def _():
        step(pl.multiple_of(start, 4 * BKT), 2 * BKT)

    @pl.when((buckets & 1) != 0)
    def _():
        step(pl.multiple_of(start + (buckets & 2) * BKT, BKT), BKT)


def load_keys(own_k, sib_k, own_v, sib_v, keys, vals):
    keys[0], keys[1] = own_k[...], sib_k[...]
    vals[0], vals[1] = own_v[...], sib_v[...]


def load_rows(owner, q_ref, g_ref, q_head, g_head):
    z_size, x_size, count, _ = q_ref.shape
    column = z_size * count
    lane = lax.broadcasted_iota(jnp.int32, (column, LANES), 1)
    for i in range(x_size // QRY):
        x = owner * (x_size // QRY) + i
        at = slice(i * column, (i + 1) * column)
        q_rows = q_ref[:, x].reshape(column, LANES)
        g_rows = g_ref[x].reshape(column, LANES)
        for h in range(2):
            mine = (lane < HDIM) if h == 0 else (lane >= HDIM)
            q_head[h, at, :] = jnp.where(mine, q_rows, jnp.zeros_like(q_rows))
            g_head[h, at, :] = jnp.where(mine, g_rows, jnp.zeros_like(g_rows))


def stats_kernel(info, own_k, sib_k, own_v, sib_v, q_ref, g_ref, out_ref,
                 keys, vals, q_head, g_head, top, total, dotted):
    rows = q_head.shape[1]
    load_keys(own_k, sib_k, own_v, sib_v, keys, vals)

    def passage(p, carry):
        load_rows(info[1 + p], q_ref, g_ref, q_head, g_head)
        top[...] = jnp.full(top.shape, -jnp.inf, F32)
        total[...] = jnp.zeros(total.shape, F32)
        dotted[...] = jnp.zeros(dotted.shape, F32)

        def step(start, count):
            k_part = keys[p, pl.ds(start, count), :]
            v_part = vals[p, pl.ds(start, count), :]
            for h in range(2):
                scores = dot_nt(k_part, q_head[h]).reshape(count // 8, 8, rows)
                upstream = dot_nt(v_part, g_head[h]).reshape(count // 8, 8, rows)
                old = top[h]
                new = jnp.maximum(old, jnp.max(scores, axis=0))
                weights = jnp.exp(scores - new[None])
                factor = jnp.exp(old - new)
                top[h] = new
                total[h] = total[h] * factor + jnp.sum(weights, axis=0)
                dotted[h] = dotted[h] * factor + jnp.sum(weights * upstream, axis=0)

        over_chunks(info[3 + p], step)
        half = rows // 2
        for h in range(2):
            peak = jnp.max(top[h], axis=0, keepdims=True)
            factor = jnp.exp(top[h] - peak)
            stats = (
                peak,
                jnp.sum(total[h] * factor, axis=0, keepdims=True),
                jnp.sum(dotted[h] * factor, axis=0, keepdims=True),
                jnp.full((1, rows), info[1 + p].astype(F32)),
            )
            for s in range(2):
                for t, stat in enumerate(stats):
                    out_ref[2 * h + s, pl.ds(2 * t + p, 1), :] = stat[:, s * half:(s + 1) * half]
        return carry

    lax.fori_loop(0, 2, passage, 0)


def merge_kernel(in_ref, out_ref):
    chips = in_ref.shape[0]
    merged = []
    tops = [in_ref[:, t, :] for t in range(2)]
    sums = [in_ref[:, 2 + t, :] for t in range(2)]
    dots = [in_ref[:, 4 + t, :] for t in range(2)]
    owners = [in_ref[:, 6 + t, :] for t in range(2)]
    for query in range(QRY):
        held = [jnp.where(owners[t] == query, tops[t], -jnp.inf) for t in range(2)]
        peak = jnp.max(jnp.maximum(held[0], held[1]), axis=0, keepdims=True)
        factors = [jnp.exp(held[t] - peak) for t in range(2)]
        total = jnp.sum(sums[0] * factors[0] + sums[1] * factors[1], axis=0, keepdims=True)
        dotted = jnp.sum(dots[0] * factors[0] + dots[1] * factors[1], axis=0, keepdims=True)
        merged.append((peak + jnp.log(total), dotted / total))
    table = jnp.concatenate(
        [merged[0][0], merged[1][0], merged[0][1], merged[1][1]]
        + [jnp.zeros_like(merged[0][0])] * 4, axis=0
    )
    out_ref[...] = jnp.broadcast_to(table[None], out_ref.shape)


def grads_kernel(info, own_k, sib_k, own_v, sib_v, q_ref, g_ref, st_ref, *rest):
    (own_dk, sib_dk, own_dv, sib_dv, dq_ref,
     keys, vals, q_head, g_head, dkeys, dvals, turned, dq_sum) = rest[-13:]
    rows = q_head.shape[1]
    load_keys(own_k, sib_k, own_v, sib_v, keys, vals)
    dkeys[...] = jnp.zeros(dkeys.shape, BF16)
    dvals[...] = jnp.zeros(dvals.shape, BF16)
    dq_sum[...] = jnp.zeros(dq_sum.shape, F32)

    def passage(p, carry):
        owner = info[1 + p]
        load_rows(owner, q_ref, g_ref, q_head, g_head)
        turned[...] = jnp.zeros(turned.shape, F32)

        def row_stat(h, t):
            return jnp.concatenate(
                [st_ref[2 * h + s, pl.ds(2 * t + owner, 1), :] for s in range(2)], axis=1
            )

        def step(start, count):
            at = pl.ds(start, count)
            k_part, v_part = keys[p, at, :], vals[p, at, :]
            k_turned = k_part.T
            dk_part = dv_part = None
            for h in range(2):
                probs = jnp.exp(dot_nt(k_part, q_head[h]) - row_stat(h, 0))
                dscore = (probs * (dot_nt(v_part, g_head[h]) - row_stat(h, 1))).astype(BF16)
                dv_term = dot_nn(probs.astype(BF16), g_head[h])
                dk_term = dot_nn(dscore, q_head[h])
                dv_part = dv_term if h == 0 else dv_part + dv_term
                dk_part = dk_term if h == 0 else dk_part + dk_term
                own = slice(h * HDIM, (h + 1) * HDIM)
                turned[own, :] += dot_nn(k_turned[own, :], dscore)
            dkeys[p, at, :] = dk_part.astype(BF16)
            dvals[p, at, :] = dv_part.astype(BF16)

        over_chunks(info[3 + p], step)
        at = pl.ds(pl.multiple_of(owner * rows, rows), rows)
        dq_sum[at, :] += turned[...].T
        return carry

    lax.fori_loop(0, 2, passage, 0)
    own_dk[...], sib_dk[...] = dkeys[0], dkeys[1]
    own_dv[...], sib_dv[...] = dvals[0], dvals[1]
    dq_ref[...] = dq_sum[...].astype(BF16)


def blocks(slots, pairs, q_shape, rows, first):
    z_size, x_size, count, _ = q_shape
    own = pl.BlockSpec((slots, LANES), lambda i, info: (0, info[0] * pairs + first + i))
    sib = pl.BlockSpec((slots, LANES), lambda i, info: (0, first + i))
    q_block = pl.BlockSpec((z_size, x_size, count, LANES), lambda i, info: (0, 0, 0, first + i))
    g_block = pl.BlockSpec((x_size, z_size, count, LANES), lambda i, info: (0, 0, 0, first + i))
    stat = pl.BlockSpec((4, 8, rows // 2), lambda i, info: (first + i, 0, 0))
    return own, [own, sib, own, sib, q_block, g_block], stat


def sizes(operands):
    info, keys, sib_k, values, sib_v, whole_q, whole_g = operands
    slots, half = sib_k.shape
    all_rows = whole_q.shape[0] * whole_q.shape[1] * whole_q.shape[2]
    return slots, half, half // LANES, all_rows, all_rows // QRY


LIMIT = pltpu.CompilerParams(
    dimension_semantics=("arbitrary",), vmem_limit_bytes=48 * 1024 * 1024
)


def key_scratch(slots):
    return [pltpu.VMEM((2, slots, LANES), BF16)] * 2


def row_stats(operands):
    slots, half, pairs, all_rows, rows = sizes(operands)
    own, in_blocks, stat = blocks(slots, pairs, operands[5].shape, rows, 0)
    return pl.pallas_call(
        stats_kernel,
        grid_spec=pltpu.PrefetchScalarGridSpec(
            num_scalar_prefetch=1,
            grid=(pairs,),
            in_specs=in_blocks,
            out_specs=stat,
            scratch_shapes=key_scratch(slots)
            + [pltpu.VMEM((2, rows, LANES), BF16)] * 2
            + [pltpu.VMEM((2, 8, rows), F32)] * 3,
        ),
        out_shape=jax.ShapeDtypeStruct((4 * pairs, 8, rows // 2), F32),
        compiler_params=LIMIT,
        cost_estimate=pl.CostEstimate(
            flops=4 * slots * rows * half * 2, bytes_accessed=10 << 20,
            transcendentals=slots * rows * half // HDIM * 2,
        ),
        name="row_stats",
    )(*operands)


def merge_stats(stats):
    return pl.pallas_call(
        merge_kernel,
        out_shape=jax.ShapeDtypeStruct(stats.shape, F32),
        in_specs=[pl.BlockSpec(memory_space=pltpu.VMEM)],
        out_specs=pl.BlockSpec(memory_space=pltpu.VMEM),
        name="merge_stats",
    )(stats)


def gradients(operands, stats, first, count, begun):
    slots, half, pairs, all_rows, rows = sizes(operands)
    own, in_blocks, stat = blocks(slots, pairs, operands[5].shape, rows, first)
    sib = pl.BlockSpec((slots, LANES), lambda i, info: (0, i))
    whole = jax.ShapeDtypeStruct((slots, 2 * half), BF16)
    part = jax.ShapeDtypeStruct((slots, count * LANES), BF16)
    given = list(begun)
    return pl.pallas_call(
        grads_kernel,
        grid_spec=pltpu.PrefetchScalarGridSpec(
            num_scalar_prefetch=1,
            grid=(count,),
            in_specs=in_blocks + [stat] + [pl.BlockSpec(memory_space=pl.ANY)] * len(given),
            out_specs=[own, sib, own, sib, pl.BlockSpec((all_rows, LANES), lambda i, info: (0, i))],
            scratch_shapes=key_scratch(slots)
            + [pltpu.VMEM((2, rows, LANES), BF16)] * 2
            + key_scratch(slots)
            + [pltpu.VMEM((LANES, rows), F32), pltpu.VMEM((all_rows, LANES), F32)],
        ),
        out_shape=[whole, part, whole, part,
                   jax.ShapeDtypeStruct((all_rows, count * LANES), BF16)],
        input_output_aliases={8: 0, 9: 2} if given else {},
        compiler_params=LIMIT,
        cost_estimate=pl.CostEstimate(
            flops=10 * slots * rows * count * LANES * 2, bytes_accessed=8 << 20,
            transcendentals=slots * rows * count * 4,
        ),
        name="gradients",
    )(*operands, stats, *given)


PARTS = 2


def per_device(x_size, z_size, queries, keys, values, grad_out, lengths, slot_query):
    chips = x_size * z_size
    core = lax.axis_index("core")
    width = keys.shape[2]
    half = width // 2
    keys, values = keys[0], values[0]

    mine = jnp.concatenate([slot_query, lengths])
    theirs = swap_cores(mine)
    info = jnp.stack([core, mine[0], theirs[0], mine[1], theirs[1]]).astype(jnp.int32)

    def features(value, of_core):
        return lax.dynamic_slice_in_dim(value, of_core * half, half, value.ndim - 1)

    both = lax.all_gather(jnp.stack([queries, grad_out]), "core", axis=1, tiled=True)
    both = features(both, core)
    whole_q = gather_x_then_z(both[0], x_size)
    whole_g = gather_z_then_x(both[1], x_size, z_size)
    sib_k = swap_cores(features(keys, 1 - core))
    sib_v = swap_cores(features(values, 1 - core))
    operands = (info, keys, sib_k, values, sib_v, whole_q, whole_g)
    slots, half, pairs, all_rows, rows = sizes(operands)

    stats = lax.all_to_all(row_stats(operands), CHIP, 0, 0, tiled=True)
    stats = lax.all_to_all(merge_stats(stats), CHIP, 0, 0, tiled=True)

    count = pairs // PARTS
    span = count * LANES
    held = all_rows // chips
    own_rows = held // 2
    begun, sibs, sums = [], [], []
    for part in range(PARTS):
        own_dk, sib_dk, own_dv, sib_dv, dq = gradients(operands, stats, part * count, count, begun)
        begun = [own_dk, own_dv]
        sibs.append((swap_cores(sib_dk), swap_cores(sib_dv)))
        terms = lax.all_to_all(dq.reshape(chips, held, span), CHIP, 0, 0, tiled=True)
        sums.append(jnp.sum(terms.astype(F32), axis=0).astype(BF16))

    own_dk, own_dv = begun
    for part, (sib_dk, sib_dv) in enumerate(sibs):
        at = (1 - core) * half + part * span
        own_dk = lax.dynamic_update_slice_in_dim(own_dk, sib_dk, at, 1)
        own_dv = lax.dynamic_update_slice_in_dim(own_dv, sib_dv, at, 1)

    summed = jnp.concatenate(sums, axis=1)
    kept = lax.dynamic_slice_in_dim(summed, core * own_rows, own_rows, 0)
    given = swap_cores(lax.dynamic_slice_in_dim(summed, (1 - core) * own_rows, own_rows, 0))
    grad_queries = jnp.where(
        core == 0, jnp.concatenate([kept, given], 1), jnp.concatenate([given, kept], 1)
    )
    return grad_queries, own_dk[None], own_dv[None]


def solution(mesh):
    groups = mesh.devices.shape[0]
    x_size, z_size = 4, 8
    fine = Mesh(
        mesh.devices.reshape(groups, x_size, z_size, 2), ("group", "x", "z", "core")
    )
    at = ("group", "x", "z", "core")
    return jax.shard_map(
        functools.partial(per_device, x_size, z_size),
        mesh=fine,
        in_specs=(P(at, None), P(at, None, None), P(at, None, None), P(at, None), P(at), P(at)),
        out_specs=(P(at, None), P(at, None, None), P(at, None, None)),
        check_vma=False,
    )
```

```python
import functools

import jax
import jax.numpy as jnp
from jax import lax
from jax.experimental import pallas as pl
from jax.experimental.pallas import tpu as pltpu
from jax.sharding import Mesh
from jax.sharding import PartitionSpec as P

HDIM = 64
BKT = 64
QRY = 2
LANES = 128
F32 = jnp.float32
BF16 = jnp.bfloat16
CHIP = ("x", "z")


def swap_cores(value):
    return lax.ppermute(value, "core", [(0, 1), (1, 0)])


def repeated(value, count):
    return jnp.broadcast_to(value[None], (count,) + value.shape)


def gather_x_then_z(value, x_size):
    columns = lax.all_to_all(repeated(value, x_size), "x", 0, 0, tiled=True)
    return lax.all_gather(columns, "z", axis=0, tiled=False)


def gather_z_then_x(value, x_size, z_size):
    column = lax.all_to_all(repeated(value, z_size), "z", 0, 0, tiled=True)
    return lax.all_to_all(repeated(column, x_size), "x", 0, 0, tiled=True)


def dot_nt(a, b):
    return lax.dot_general(a, b, (((1,), (1,)), ((), ())), preferred_element_type=F32)


def dot_nn(a, b):
    return lax.dot_general(a, b, (((1,), (0,)), ((), ())), preferred_element_type=F32)


def by_length(buckets, step):
    for most in range(2, 9, 2):

        @pl.when((buckets == most) | (buckets == most - 1))
        def _():
            step(most * BKT, buckets == most)


def masked(scores, tail_used):
    cut = scores.shape[0] - BKT
    tail = jnp.where(tail_used, scores[cut:], -jnp.inf)
    return jnp.concatenate([scores[:cut], tail], axis=0)


def load_keys(own_k, sib_k, own_v, sib_v, keys, vals):
    keys[0], keys[1] = own_k[...], sib_k[...]
    vals[0], vals[1] = own_v[...], sib_v[...]


def load_rows(z_first, owner, q_ref, g_ref, q_head, g_head):
    z_size, x_size = q_ref.shape[:2] if z_first else q_ref.shape[1::-1]
    column = z_size * q_ref.shape[3]
    lane = lax.broadcasted_iota(jnp.int32, (column, LANES), 1)
    for i in range(x_size // QRY):
        x = owner * (x_size // QRY) + i
        at = slice(i * column, (i + 1) * column)
        for ref, head in ((q_ref, q_head), (g_ref, g_head)):
            value = (ref[:, x, 0] if z_first else ref[x, :, 0]).reshape(column, LANES)
            for h in range(2):
                mine = (lane < HDIM) if h == 0 else (lane >= HDIM)
                head[h, at, :] = jnp.where(mine, value, jnp.zeros_like(value))


def over_pairs(body, info, wide, narrow, rest):
    count = wide[0].shape[-1] // LANES

    def pair(j, carry):
        lanes = pl.ds(pl.multiple_of(j * LANES, LANES), LANES)
        views = [ref.at[(slice(None),) * (len(ref.shape) - 1) + (lanes,)] for ref in wide]
        body(info, views, narrow.at[pl.ds(4 * j, 4)], *rest)
        return carry

    lax.fori_loop(0, count, pair, 0)


def stats_kernel(z_first, info, own_k, sib_k, own_v, sib_v, q_ref, g_ref, *rest):
    out_ref, scratch = rest[-5], rest[-4:]
    wide = [own_k, sib_k, own_v, sib_v, q_ref, g_ref]
    over_pairs(functools.partial(stats_pair, z_first), info, wide, out_ref, scratch)


def stats_pair(z_first, info, views, out_ref, keys, vals, q_head, g_head):
    own_k, sib_k, own_v, sib_v, q_ref, g_ref = views
    rows = q_head.shape[1]
    half = rows // 2
    load_keys(own_k, sib_k, own_v, sib_v, keys, vals)

    def passage(p, carry):
        load_rows(z_first, info[1 + p], q_ref, g_ref, q_head, g_head)

        def step(count, tail_used):
            k_part, v_part = keys[p, :count, :], vals[p, :count, :]
            heads = [(h, slice(s * half, (s + 1) * half)) for h in range(2) for s in range(2)]
            scores = [masked(dot_nt(k_part, q_head[h, at, :]), tail_used) for h, at in heads]
            upstream = [dot_nt(v_part, g_head[h, at, :]) for h, at in heads]
            for n in range(4):
                peak = jnp.max(scores[n], axis=0, keepdims=True)
                weights = jnp.exp(scores[n] - peak)
                stats = (
                    peak,
                    jnp.sum(weights, axis=0, keepdims=True),
                    jnp.sum(weights * upstream[n], axis=0, keepdims=True),
                    jnp.full((1, half), info[1 + p].astype(F32)),
                )
                for t, stat in enumerate(stats):
                    out_ref[n, pl.ds(2 * t + p, 1), :] = stat

        by_length(info[3 + p], step)
        return carry

    lax.fori_loop(0, 2, passage, 0)


def merge_kernel(in_ref, out_ref):
    chips = in_ref.shape[0]
    merged = []
    tops = [in_ref[:, t, :] for t in range(2)]
    sums = [in_ref[:, 2 + t, :] for t in range(2)]
    dots = [in_ref[:, 4 + t, :] for t in range(2)]
    owners = [in_ref[:, 6 + t, :] for t in range(2)]
    for query in range(QRY):
        held = [jnp.where(owners[t] == query, tops[t], -jnp.inf) for t in range(2)]
        peak = jnp.max(jnp.maximum(held[0], held[1]), axis=0, keepdims=True)
        factors = [jnp.exp(held[t] - peak) for t in range(2)]
        total = jnp.sum(sums[0] * factors[0] + sums[1] * factors[1], axis=0, keepdims=True)
        dotted = jnp.sum(dots[0] * factors[0] + dots[1] * factors[1], axis=0, keepdims=True)
        merged.append((peak + jnp.log(total), dotted / total))
    table = jnp.concatenate(
        [merged[0][0], merged[1][0], merged[0][1], merged[1][1]]
        + [jnp.zeros_like(merged[0][0])] * 4, axis=0
    )
    out_ref[...] = jnp.broadcast_to(table[None], out_ref.shape)


def grads_kernel(z_first, info, own_k, sib_k, own_v, sib_v, q_ref, g_ref, st_ref, *rest):
    outs, scratch = rest[-13:-8], rest[-8:]
    wide = [own_k, sib_k, own_v, sib_v, q_ref, g_ref, *outs]
    over_pairs(functools.partial(grads_pair, z_first), info, wide, st_ref, scratch)


def grads_pair(z_first, info, views, st_ref,
               keys, vals, q_head, g_head, dkeys, dvals, turned, dq_sum):
    (own_k, sib_k, own_v, sib_v, q_ref, g_ref,
     own_dk, sib_dk, own_dv, sib_dv, dq_ref) = views
    rows = q_head.shape[1]
    load_keys(own_k, sib_k, own_v, sib_v, keys, vals)
    dkeys[...] = jnp.zeros(dkeys.shape, BF16)
    dvals[...] = jnp.zeros(dvals.shape, BF16)
    dq_sum[...] = jnp.zeros(dq_sum.shape, F32)

    def passage(p, carry):
        owner = info[1 + p]
        load_rows(z_first, owner, q_ref, g_ref, q_head, g_head)

        def row_stat(h, t):
            return jnp.concatenate(
                [st_ref[2 * h + s, pl.ds(2 * t + owner, 1), :] for s in range(2)], axis=1
            )

        def step(count, tail_used):
            k_part, v_part = keys[p, :count, :], vals[p, :count, :]
            k_turned = k_part.T
            half = rows // 2
            heads = [(h, slice(s * half, (s + 1) * half)) for h in range(2) for s in range(2)]
            scores = [masked(dot_nt(k_part, q_head[h, at, :]), tail_used) for h, at in heads]
            upstream = [dot_nt(v_part, g_head[h, at, :]) for h, at in heads]
            probs = [jnp.exp(scores[n] - st_ref[n, pl.ds(owner, 1), :]) for n in range(4)]
            dscore = [(probs[n] * (upstream[n] - st_ref[n, pl.ds(2 + owner, 1), :])).astype(BF16) for n in range(4)]
            low = jnp.concatenate([x.astype(BF16) for x in probs], axis=1)
            dv_part = dot_nn(low, g_head[...].reshape(2 * rows, LANES))
            dk_part = dot_nn(jnp.concatenate(dscore, axis=1), q_head[...].reshape(2 * rows, LANES))
            dscore = [jnp.concatenate(dscore[2 * h:2 * h + 2], axis=1) for h in range(2)]
            for h in range(2):
                own = slice(h * HDIM, (h + 1) * HDIM)
                turned[own, :] = dot_nn(k_turned[own, :], dscore[h])
            dkeys[p, :count, :] = dk_part.astype(BF16)
            dvals[p, :count, :] = dv_part.astype(BF16)

        by_length(info[3 + p], step)
        at = pl.ds(pl.multiple_of(owner * rows, rows), rows)
        dq_sum[at, :] += turned[...].T
        return carry

    lax.fori_loop(0, 2, passage, 0)
    own_dk[...], sib_dk[...] = dkeys[0], dkeys[1]
    own_dv[...], sib_dv[...] = dvals[0], dvals[1]
    dq_ref[...] = dq_sum[...].astype(BF16)


PARTS = 2
PAIRS_A_STEP = 1


def blocks(slots, pairs, shape, part):
    span = PAIRS_A_STEP * LANES
    steps = pairs // PAIRS_A_STEP
    first = part * (steps // PARTS)
    own = pl.BlockSpec((slots, span), lambda i, info: (0, info[0] * steps + first + i))
    sib = pl.BlockSpec((slots, span), lambda i, info: (0, first + i))
    q_block = pl.BlockSpec(shape[:2] + (1, shape[3], span), lambda i, info: (0, 0, 0, 0, i))
    g_block = pl.BlockSpec(shape[:2] + (1, shape[3], span), lambda i, info: (0, 0, 1, 0, i))
    return own, [own, sib, own, sib, q_block, g_block], first, steps // PARTS


def sizes(operands):
    slots, half = operands[2].shape
    shape = operands[5].shape
    all_rows = shape[0] * shape[1] * shape[3]
    return slots, half, half // LANES, all_rows, all_rows // QRY


LIMIT = pltpu.CompilerParams(
    dimension_semantics=("arbitrary",), vmem_limit_bytes=48 * 1024 * 1024
)


def key_scratch(slots):
    return [pltpu.VMEM((2, slots, LANES), BF16)] * 2


def row_stats(operands, part, begun):
    slots, half, pairs, all_rows, rows = sizes(operands)
    own, in_blocks, first, steps = blocks(slots, pairs, operands[5].shape, part)
    return pl.pallas_call(
        functools.partial(stats_kernel, part == 0),
        grid_spec=pltpu.PrefetchScalarGridSpec(
            num_scalar_prefetch=1,
            grid=(steps,),
            in_specs=in_blocks + [pl.BlockSpec(memory_space=pl.ANY)] * len(begun),
            out_specs=pl.BlockSpec(
                (4 * PAIRS_A_STEP, 8, rows // 2), lambda i, info: (first + i, 0, 0)
            ),
            scratch_shapes=key_scratch(slots) + [pltpu.VMEM((2, rows, LANES), BF16)] * 2,
        ),
        out_shape=jax.ShapeDtypeStruct((4 * pairs, 8, rows // 2), F32),
        input_output_aliases={7: 0} if begun else {},
        compiler_params=LIMIT,
        cost_estimate=pl.CostEstimate(
            flops=4 * slots * rows * half, bytes_accessed=5 << 20,
            transcendentals=slots * rows * half // HDIM,
        ),
        name="row_stats",
    )(*operands, *begun)


def merge_stats(stats):
    return pl.pallas_call(
        merge_kernel,
        out_shape=jax.ShapeDtypeStruct(stats.shape, F32),
        in_specs=[pl.BlockSpec(memory_space=pltpu.VMEM)],
        out_specs=pl.BlockSpec(memory_space=pltpu.VMEM),
        name="merge_stats",
    )(stats)


def gradients(operands, stats, part, begun):
    slots, half, pairs, all_rows, rows = sizes(operands)
    own, in_blocks, first, steps = blocks(slots, pairs, operands[5].shape, part)
    span = PAIRS_A_STEP * LANES
    sib = pl.BlockSpec((slots, span), lambda i, info: (0, i))
    stat = pl.BlockSpec((4 * PAIRS_A_STEP, 8, rows // 2), lambda i, info: (first + i, 0, 0))
    whole = jax.ShapeDtypeStruct((slots, 2 * half), BF16)
    half_part = jax.ShapeDtypeStruct((slots, steps * span), BF16)
    return pl.pallas_call(
        functools.partial(grads_kernel, part == 0),
        grid_spec=pltpu.PrefetchScalarGridSpec(
            num_scalar_prefetch=1,
            grid=(steps,),
            in_specs=in_blocks + [stat] + [pl.BlockSpec(memory_space=pl.ANY)] * len(begun),
            out_specs=[own, sib, own, sib, pl.BlockSpec((all_rows, span), lambda i, info: (0, i))],
            scratch_shapes=key_scratch(slots)
            + [pltpu.VMEM((2, rows, LANES), BF16)] * 2
            + key_scratch(slots)
            + [pltpu.VMEM((LANES, rows), F32), pltpu.VMEM((all_rows, LANES), F32)],
        ),
        out_shape=[whole, half_part, whole, half_part,
                   jax.ShapeDtypeStruct((all_rows, steps * span), BF16)],
        input_output_aliases={8: 0, 9: 2} if begun else {},
        compiler_params=LIMIT,
        cost_estimate=pl.CostEstimate(
            flops=10 * slots * rows * half, bytes_accessed=8 << 20,
            transcendentals=slots * rows * half // HDIM,
        ),
        name="gradients",
    )(*operands, stats, *begun)


def per_device(x_size, z_size, queries, keys, values, grad_out, lengths, slot_query):
    chips = x_size * z_size
    core = lax.axis_index("core")
    width = keys.shape[2]
    half = width // 2
    span = half // PARTS
    keys, values = keys[0], values[0]

    mine = jnp.concatenate([slot_query, lengths])
    theirs = swap_cores(mine)
    info = jnp.stack([core, mine[0], theirs[0], mine[1], theirs[1]]).astype(jnp.int32)

    def features(value, at, count):
        return lax.dynamic_slice_in_dim(value, at, count, value.ndim - 1)

    both = lax.all_gather(jnp.stack([queries, grad_out]), "core", axis=1, tiled=True)
    gathered = (
        gather_x_then_z(features(both, core * half, span), x_size),
        gather_z_then_x(features(both, core * half + span, span), x_size, z_size),
    )
    sib_k = swap_cores(features(keys, (1 - core) * half, half))
    sib_v = swap_cores(features(values, (1 - core) * half, half))
    operands = [(info, keys, sib_k, values, sib_v, rows, rows) for rows in gathered]
    all_rows = sizes(operands[0])[3]

    stats = []
    for part in range(PARTS):
        stats = [row_stats(operands[part], part, stats)]
    stats = lax.all_to_all(stats[0], CHIP, 0, 0, tiled=True)
    stats = lax.all_to_all(merge_stats(stats), CHIP, 0, 0, tiled=True)

    held = all_rows // chips
    own_rows = held // 2
    begun, sibs, sums = [], [], []
    for part in range(PARTS):
        own_dk, sib_dk, own_dv, sib_dv, dq = gradients(operands[part], stats, part, begun)
        begun = [own_dk, own_dv]
        sibs.append((swap_cores(sib_dk), swap_cores(sib_dv)))
        terms = lax.all_to_all(dq.reshape(chips, held, span), CHIP, 0, 0, tiled=True)
        sums.append(jnp.sum(terms.astype(F32), axis=0).astype(BF16))

    own_dk, own_dv = begun
    for part, (sib_dk, sib_dv) in enumerate(sibs):
        at = (1 - core) * half + part * span
        own_dk = lax.dynamic_update_slice_in_dim(own_dk, sib_dk, at, 1)
        own_dv = lax.dynamic_update_slice_in_dim(own_dv, sib_dv, at, 1)

    summed = jnp.concatenate(sums, axis=1)
    kept = lax.dynamic_slice_in_dim(summed, core * own_rows, own_rows, 0)
    given = swap_cores(lax.dynamic_slice_in_dim(summed, (1 - core) * own_rows, own_rows, 0))
    grad_queries = jnp.where(
        core == 0, jnp.concatenate([kept, given], 1), jnp.concatenate([given, kept], 1)
    )
    return grad_queries, own_dk[None], own_dv[None]


def solution(mesh):
    groups = mesh.devices.shape[0]
    x_size, z_size = 4, 8
    fine = Mesh(
        mesh.devices.reshape(groups, x_size, z_size, 2), ("group", "x", "z", "core")
    )
    at = ("group", "x", "z", "core")
    return jax.shard_map(
        functools.partial(per_device, x_size, z_size),
        mesh=fine,
        in_specs=(P(at, None), P(at, None, None), P(at, None, None), P(at, None), P(at), P(at)),
        out_specs=(P(at, None), P(at, None, None), P(at, None, None)),
        check_vma=False,
    )
```

```python
import functools

import jax
import jax.numpy as jnp
from jax import lax
from jax.experimental import pallas as pl
from jax.experimental.pallas import tpu as pltpu
from jax.sharding import Mesh
from jax.sharding import PartitionSpec as P

HDIM = 64
BKT = 64
QRY = 2
LANES = 128
F32 = jnp.float32
BF16 = jnp.bfloat16
CHIP = ("x", "z")


def swap_cores(value):
    return lax.ppermute(value, "core", [(0, 1), (1, 0)])


def repeated(value, count):
    return jnp.broadcast_to(value[None], (count,) + value.shape)


def across(value, axes):
    flat = value.reshape((-1,) + value.shape[2:])
    return lax.all_to_all(flat, axes, 0, 0, tiled=True).reshape(value.shape)


def gather_x_then_z(value, x_size):
    columns = across(repeated(value, x_size), ("x", "core"))
    return lax.all_gather(columns, "z", axis=0, tiled=False)


def gather_z_then_x(value, x_size, z_size):
    column = across(repeated(value, z_size), ("z", "core"))
    return lax.all_to_all(repeated(column, x_size), "x", 0, 0, tiled=True)


def dot_nt(a, b):
    return lax.dot_general(a, b, (((1,), (1,)), ((), ())), preferred_element_type=F32)


def dot_nn(a, b):
    return lax.dot_general(a, b, (((1,), (0,)), ((), ())), preferred_element_type=F32)


def by_length(buckets, step):
    for most in range(2, 9, 2):

        @pl.when((buckets == most) | (buckets == most - 1))
        def _():
            step(most * BKT, buckets == most)


def masked(scores, tail_used):
    cut = scores.shape[0] - BKT
    tail = jnp.where(tail_used, scores[cut:], -jnp.inf)
    return jnp.concatenate([scores[:cut], tail], axis=0)


def load_rows(z_first, owner, q_ref, g_ref, q_head, g_head):
    z_size, x_size = q_ref.shape[:2] if z_first else q_ref.shape[1::-1]
    column = z_size * q_ref.shape[2] * q_ref.shape[4]
    lane = lax.broadcasted_iota(jnp.int32, (column, LANES), 1)
    for i in range(x_size // QRY):
        x = owner * (x_size // QRY) + i
        at = slice(i * column, (i + 1) * column)
        for ref, head in ((q_ref, q_head), (g_ref, g_head)):
            value = (ref[:, x, :, 0] if z_first else ref[x, :, :, 0]).reshape(column, LANES)
            for h in range(2):
                mine = (lane < HDIM) if h == 0 else (lane >= HDIM)
                head[h, at, :] = jnp.where(mine, value, jnp.zeros_like(value))


def with_rows(p, z_first, info, q_ref, g_ref, q_head, g_head):
    @pl.when((p == 0) | (info[1] != info[2]))
    def _():
        load_rows(z_first, info[1 + p], q_ref, g_ref, q_head, g_head)


def stats_kernel(z_first, info, own_k, sib_k, own_v, sib_v, q_ref, g_ref, *rest):
    out_ref, q_head, g_head = rest[-3:]
    rows = q_head.shape[1]
    half = rows // 2

    for p, (k_ref, v_ref) in enumerate(((own_k, own_v), (sib_k, sib_v))):
        with_rows(p, z_first, info, q_ref, g_ref, q_head, g_head)

        def step(count, tail_used, p=p, k_ref=k_ref, v_ref=v_ref):
            k_part, v_part = k_ref[:count, :], v_ref[:count, :]
            heads = [(h, slice(s * half, (s + 1) * half)) for h in range(2) for s in range(2)]
            scores = [masked(dot_nt(k_part, q_head[h, at, :]), tail_used) for h, at in heads]
            upstream = [dot_nt(v_part, g_head[h, at, :]) for h, at in heads]
            for n in range(4):
                peak = jnp.max(scores[n], axis=0, keepdims=True)
                weights = jnp.exp(scores[n] - peak)
                stats = (
                    peak,
                    jnp.sum(weights, axis=0, keepdims=True),
                    jnp.sum(weights * upstream[n], axis=0, keepdims=True),
                    jnp.full((1, half), info[1 + p].astype(F32)),
                )
                for t, stat in enumerate(stats):
                    out_ref[n, 2 * t + p:2 * t + p + 1, :] = stat

        by_length(info[3 + p], step)


def merge_kernel(in_ref, out_ref):
    chips = in_ref.shape[0]
    merged = []
    tops = [in_ref[:, t, :] for t in range(2)]
    sums = [in_ref[:, 2 + t, :] for t in range(2)]
    dots = [in_ref[:, 4 + t, :] for t in range(2)]
    owners = [in_ref[:, 6 + t, :] for t in range(2)]
    for query in range(QRY):
        held = [jnp.where(owners[t] == query, tops[t], -jnp.inf) for t in range(2)]
        peak = jnp.max(jnp.maximum(held[0], held[1]), axis=0, keepdims=True)
        factors = [jnp.exp(held[t] - peak) for t in range(2)]
        total = jnp.sum(sums[0] * factors[0] + sums[1] * factors[1], axis=0, keepdims=True)
        dotted = jnp.sum(dots[0] * factors[0] + dots[1] * factors[1], axis=0, keepdims=True)
        merged.append((peak + jnp.log(total), dotted / total))
    table = jnp.concatenate(
        [merged[0][0], merged[1][0], merged[0][1], merged[1][1]]
        + [jnp.zeros_like(merged[0][0])] * 4, axis=0
    )
    out_ref[...] = jnp.broadcast_to(table[None], out_ref.shape)


def grads_kernel(z_first, info, own_k, sib_k, own_v, sib_v, q_ref, g_ref, st_ref, *rest):
    own_dk, sib_dk, own_dv, sib_dv, dq_ref, q_head, g_head, turned = rest[-8:]
    rows = q_head.shape[1]
    half = rows // 2
    sides = ((own_k, own_v, own_dk, own_dv), (sib_k, sib_v, sib_dk, sib_dv))

    for p, refs in enumerate(sides):
        with_rows(p, z_first, info, q_ref, g_ref, q_head, g_head)

        def step(count, tail_used, p=p, refs=refs, owner=info[1 + p]):
            k_ref, v_ref, dk_ref, dv_ref = refs
            k_part, v_part = k_ref[:count, :], v_ref[:count, :]
            k_turned = k_part.T
            heads = [(h, slice(s * half, (s + 1) * half)) for h in range(2) for s in range(2)]
            scores = [masked(dot_nt(k_part, q_head[h, at, :]), tail_used) for h, at in heads]
            upstream = [dot_nt(v_part, g_head[h, at, :]) for h, at in heads]
            probs = [jnp.exp(scores[n] - st_ref[n, pl.ds(owner, 1), :]) for n in range(4)]
            dscore = [
                (probs[n] * (upstream[n] - st_ref[n, pl.ds(2 + owner, 1), :])).astype(BF16)
                for n in range(4)
            ]
            low = jnp.concatenate([x.astype(BF16) for x in probs], axis=1)
            dv_part = dot_nn(low, g_head[...].reshape(2 * rows, LANES))
            dk_part = dot_nn(jnp.concatenate(dscore, axis=1), q_head[...].reshape(2 * rows, LANES))
            for h in range(2):
                own = slice(h * HDIM, (h + 1) * HDIM)
                both = jnp.concatenate(dscore[2 * h:2 * h + 2], axis=1)
                turned[p, own, :] = dot_nn(k_turned[own, :], both)
            for ref, part in ((dk_ref, dk_part), (dv_ref, dv_part)):
                ref[:count, :] = part.astype(BF16)
                unused = ref.shape[0] - count
                if unused:
                    ref[count:, :] = jnp.zeros((unused, LANES), BF16)

        by_length(info[3 + p], step)

    first = pl.ds(pl.multiple_of(info[1] * rows, rows), rows)
    other = pl.ds(pl.multiple_of((1 - info[1]) * rows, rows), rows)
    same = info[1] == info[2]

    @pl.when(same)
    def _():
        dq_ref[first, :] = (turned[0] + turned[1]).astype(BF16).T
        dq_ref[other, :] = jnp.zeros((rows, LANES), BF16)

    @pl.when(jnp.logical_not(same))
    def _():
        dq_ref[first, :] = turned[0].astype(BF16).T
        dq_ref[other, :] = turned[1].astype(BF16).T


PARTS = 2


def blocks(slots, pairs, shape, part):
    span, steps = LANES, pairs
    first = part * (steps // PARTS)
    own = pl.BlockSpec((slots, span), lambda i, info: (0, info[0] * steps + first + i))
    sib = pl.BlockSpec((slots, span), lambda i, info: (0, first + i))
    q_block, g_block = (
        pl.BlockSpec(shape[:3] + (1, shape[4], span), lambda i, info, t=t: (0, 0, 0, t, 0, i))
        for t in range(2)
    )
    return own, [own, sib, own, sib, q_block, g_block], first, steps // PARTS


def sizes(operands):
    slots, half = operands[2].shape
    shape = operands[5].shape
    all_rows = shape[0] * shape[1] * shape[2] * shape[4]
    return slots, half, half // LANES, all_rows, all_rows // QRY


LIMIT = pltpu.CompilerParams(
    dimension_semantics=("arbitrary",), vmem_limit_bytes=48 * 1024 * 1024
)


def row_stats(operands, part, begun):
    slots, half, pairs, all_rows, rows = sizes(operands)
    own, in_blocks, first, steps = blocks(slots, pairs, operands[5].shape, part)
    return pl.pallas_call(
        functools.partial(stats_kernel, part == 0),
        grid_spec=pltpu.PrefetchScalarGridSpec(
            num_scalar_prefetch=1,
            grid=(steps,),
            in_specs=in_blocks + [pl.BlockSpec(memory_space=pl.ANY)] * len(begun),
            out_specs=pl.BlockSpec(
                (4, 8, rows // 2), lambda i, info: (first + i, 0, 0)
            ),
            scratch_shapes=[pltpu.VMEM((2, rows, LANES), BF16)] * 2,
        ),
        out_shape=jax.ShapeDtypeStruct((4 * pairs, 8, rows // 2), F32),
        input_output_aliases={7: 0} if begun else {},
        compiler_params=LIMIT,
        cost_estimate=pl.CostEstimate(
            flops=4 * slots * rows * half, bytes_accessed=5 << 20,
            transcendentals=slots * rows * half // HDIM,
        ),
        name="row_stats",
    )(*operands, *begun)


def merge_stats(stats):
    return pl.pallas_call(
        merge_kernel,
        out_shape=jax.ShapeDtypeStruct(stats.shape, F32),
        in_specs=[pl.BlockSpec(memory_space=pltpu.VMEM)],
        out_specs=pl.BlockSpec(memory_space=pltpu.VMEM),
        name="merge_stats",
    )(stats)


def gradients(operands, stats, part, begun):
    slots, half, pairs, all_rows, rows = sizes(operands)
    own, in_blocks, first, steps = blocks(slots, pairs, operands[5].shape, part)
    span = LANES
    sib = pl.BlockSpec((slots, span), lambda i, info: (0, i))
    stat = pl.BlockSpec((4, 8, rows // 2), lambda i, info: (first + i, 0, 0))
    whole = jax.ShapeDtypeStruct((slots, 2 * half), BF16)
    half_part = jax.ShapeDtypeStruct((slots, steps * span), BF16)
    return pl.pallas_call(
        functools.partial(grads_kernel, part == 0),
        grid_spec=pltpu.PrefetchScalarGridSpec(
            num_scalar_prefetch=1,
            grid=(steps,),
            in_specs=in_blocks + [stat] + [pl.BlockSpec(memory_space=pl.ANY)] * len(begun),
            out_specs=[own, sib, own, sib, pl.BlockSpec((all_rows, span), lambda i, info: (0, i))],
            scratch_shapes=[pltpu.VMEM((2, rows, LANES), BF16)] * 2
            + [pltpu.VMEM((2, LANES, rows), F32)],
        ),
        out_shape=[whole, half_part, whole, half_part,
                   jax.ShapeDtypeStruct((all_rows, steps * span), BF16)],
        input_output_aliases={8: 0, 9: 2} if begun else {},
        compiler_params=LIMIT,
        cost_estimate=pl.CostEstimate(
            flops=10 * slots * rows * half, bytes_accessed=8 << 20,
            transcendentals=slots * rows * half // HDIM,
        ),
        name="gradients",
    )(*operands, stats, *begun)


def per_device(x_size, z_size, queries, keys, values, grad_out, lengths, slot_query):
    chips = x_size * z_size
    core = lax.axis_index("core")
    width = keys.shape[2]
    half = width // 2
    span = half // PARTS
    keys, values = keys[0], values[0]

    mine = jnp.concatenate([slot_query, lengths])
    theirs = swap_cores(mine)
    info = jnp.stack([core, mine[0], theirs[0], mine[1], theirs[1]]).astype(jnp.int32)

    def features(value, at, count):
        return lax.dynamic_slice_in_dim(value, at, count, value.ndim - 1)

    own = []
    for part in range(PARTS):
        cuts = [
            lax.slice_in_dim(value, c * half + part * span, c * half + (part + 1) * span, axis=1)
            for c in range(2) for value in (queries, grad_out)
        ]
        own.append(jnp.concatenate(cuts, axis=0).reshape(2, 2, queries.shape[0], span))
    gathered = (
        gather_x_then_z(own[0], x_size),
        gather_z_then_x(own[1], x_size, z_size),
    )
    sib_k = swap_cores(features(keys, (1 - core) * half, half))
    sib_v = swap_cores(features(values, (1 - core) * half, half))
    operands = [(info, keys, sib_k, values, sib_v, rows, rows) for rows in gathered]
    all_rows = sizes(operands[0])[3]

    stats = []
    for part in range(PARTS):
        stats = [row_stats(operands[part], part, stats)]
    stats = lax.all_to_all(stats[0], CHIP, 0, 0, tiled=True)
    stats = lax.all_to_all(merge_stats(stats), CHIP, 0, 0, tiled=True)

    held = all_rows // chips
    own_rows = held // 2
    begun, sibs, sums = [], [], []
    for part in range(PARTS):
        own_dk, sib_dk, own_dv, sib_dv, dq = gradients(operands[part], stats, part, begun)
        begun = [own_dk, own_dv]
        sibs.append((swap_cores(sib_dk), swap_cores(sib_dv)))
        terms = lax.all_to_all(dq.reshape(chips, held, span), CHIP, 0, 0, tiled=True)
        sums.append(jnp.sum(terms.astype(F32), axis=0).astype(BF16))

    own_dk, own_dv = begun
    for part, (sib_dk, sib_dv) in enumerate(sibs):
        at = (1 - core) * half + part * span
        own_dk = lax.dynamic_update_slice_in_dim(own_dk, sib_dk, at, 1)
        own_dv = lax.dynamic_update_slice_in_dim(own_dv, sib_dv, at, 1)

    summed = jnp.concatenate(sums, axis=1)
    kept = lax.dynamic_slice_in_dim(summed, core * own_rows, own_rows, 0)
    given = swap_cores(lax.dynamic_slice_in_dim(summed, (1 - core) * own_rows, own_rows, 0))
    grad_queries = jnp.where(
        core == 0, jnp.concatenate([kept, given], 1), jnp.concatenate([given, kept], 1)
    )
    return grad_queries, own_dk[None], own_dv[None]


def solution(mesh):
    groups = mesh.devices.shape[0]
    x_size, z_size = 4, 8
    fine = Mesh(
        mesh.devices.reshape(groups, x_size, z_size, 2), ("group", "x", "z", "core")
    )
    at = ("group", "x", "z", "core")
    return jax.shard_map(
        functools.partial(per_device, x_size, z_size),
        mesh=fine,
        in_specs=(P(at, None), P(at, None, None), P(at, None, None), P(at, None), P(at), P(at)),
        out_specs=(P(at, None), P(at, None, None), P(at, None, None)),
        check_vma=False,
    )
```

```python
import functools

import jax
import jax.numpy as jnp
from jax import lax
from jax.experimental import pallas as pl
from jax.experimental.pallas import tpu as pltpu
from jax.sharding import Mesh
from jax.sharding import PartitionSpec as P

HDIM = 64
BKT = 64
QRY = 2
LANES = 128
F32 = jnp.float32
BF16 = jnp.bfloat16
CHIP = ("x", "z")


def swap_cores(value):
    return lax.ppermute(value, "core", [(0, 1), (1, 0)])


def repeated(value, count):
    return jnp.broadcast_to(value[None], (count,) + value.shape)


def gather_x_then_z(value, x_size):
    columns = lax.all_to_all(repeated(value, x_size), "x", 0, 0, tiled=True)
    return lax.all_gather(columns, "z", axis=0, tiled=False)


def gather_z_then_x(value, x_size, z_size):
    column = lax.all_to_all(repeated(value, z_size), "z", 0, 0, tiled=True)
    return lax.all_to_all(repeated(column, x_size), "x", 0, 0, tiled=True)


def dot_nt(a, b):
    return lax.dot_general(a, b, (((1,), (1,)), ((), ())), preferred_element_type=F32)


def dot_nn(a, b):
    return lax.dot_general(a, b, (((1,), (0,)), ((), ())), preferred_element_type=F32)


def by_length(buckets, step):
    for most in range(2, 9, 2):

        @pl.when((buckets == most) | (buckets == most - 1))
        def _():
            step(most * BKT, buckets == most)


def masked(scores, tail_used):
    cut = scores.shape[0] - BKT
    tail = jnp.where(tail_used, scores[cut:], -jnp.inf)
    return jnp.concatenate([scores[:cut], tail], axis=0)


def load_rows(z_first, owner, q_ref, g_ref, q_head, g_head):
    z_size, x_size = q_ref.shape[:2] if z_first else q_ref.shape[1::-1]
    column = z_size * q_ref.shape[2] * q_ref.shape[4]
    lane = lax.broadcasted_iota(jnp.int32, (column, LANES), 1)
    for i in range(x_size // QRY):
        x = owner * (x_size // QRY) + i
        at = slice(i * column, (i + 1) * column)
        for ref, head in ((q_ref, q_head), (g_ref, g_head)):
            value = (ref[:, x, :, 0] if z_first else ref[x, :, :, 0]).reshape(column, LANES)
            for h in range(2):
                mine = (lane < HDIM) if h == 0 else (lane >= HDIM)
                head[h, at, :] = jnp.where(mine, value, jnp.zeros_like(value))


def with_rows(p, z_first, info, q_ref, g_ref, q_head, g_head):
    @pl.when((p == 0) | (info[1] != info[2]))
    def _():
        load_rows(z_first, info[1 + p], q_ref, g_ref, q_head, g_head)


def stats_kernel(z_first, info, own_k, sib_k, own_v, sib_v, q_ref, g_ref, *rest):
    out_ref, q_head, g_head = rest[-3:]
    rows = q_head.shape[1]
    half = rows // 2

    for p, (k_ref, v_ref) in enumerate(((own_k, own_v), (sib_k, sib_v))):
        with_rows(p, z_first, info, q_ref, g_ref, q_head, g_head)

        def step(count, tail_used, p=p, k_ref=k_ref, v_ref=v_ref):
            k_part, v_part = k_ref[:count, :], v_ref[:count, :]
            heads = [(h, slice(s * half, (s + 1) * half)) for h in range(2) for s in range(2)]
            scores = [masked(dot_nt(k_part, q_head[h, at, :]), tail_used) for h, at in heads]
            upstream = [dot_nt(v_part, g_head[h, at, :]) for h, at in heads]
            for n in range(4):
                peak = jnp.max(scores[n], axis=0, keepdims=True)
                weights = jnp.exp(scores[n] - peak)
                stats = (
                    peak,
                    jnp.sum(weights, axis=0, keepdims=True),
                    jnp.sum(weights * upstream[n], axis=0, keepdims=True),
                    jnp.full((1, half), info[1 + p].astype(F32)),
                )
                for t, stat in enumerate(stats):
                    out_ref[n, 2 * t + p:2 * t + p + 1, :] = stat

        by_length(info[3 + p], step)


def merge_kernel(in_ref, out_ref):
    chips = in_ref.shape[0]
    merged = []
    tops = [in_ref[:, t, :] for t in range(2)]
    sums = [in_ref[:, 2 + t, :] for t in range(2)]
    dots = [in_ref[:, 4 + t, :] for t in range(2)]
    owners = [in_ref[:, 6 + t, :] for t in range(2)]
    for query in range(QRY):
        held = [jnp.where(owners[t] == query, tops[t], -jnp.inf) for t in range(2)]
        peak = jnp.max(jnp.maximum(held[0], held[1]), axis=0, keepdims=True)
        factors = [jnp.exp(held[t] - peak) for t in range(2)]
        total = jnp.sum(sums[0] * factors[0] + sums[1] * factors[1], axis=0, keepdims=True)
        dotted = jnp.sum(dots[0] * factors[0] + dots[1] * factors[1], axis=0, keepdims=True)
        merged.append((peak + jnp.log(total), dotted / total))
    table = jnp.concatenate(
        [merged[0][0], merged[1][0], merged[0][1], merged[1][1]]
        + [jnp.zeros_like(merged[0][0])] * 4, axis=0
    )
    out_ref[...] = jnp.broadcast_to(table[None], out_ref.shape)


def grads_kernel(z_first, info, own_k, sib_k, own_v, sib_v, q_ref, g_ref, st_ref, *rest):
    own_dk, sib_dk, own_dv, sib_dv, dq_ref, q_head, g_head, turned = rest[-8:]
    rows = q_head.shape[1]
    half = rows // 2
    sides = ((own_k, own_v, own_dk, own_dv), (sib_k, sib_v, sib_dk, sib_dv))

    for p, refs in enumerate(sides):
        with_rows(p, z_first, info, q_ref, g_ref, q_head, g_head)

        def step(count, tail_used, p=p, refs=refs, owner=info[1 + p]):
            k_ref, v_ref, dk_ref, dv_ref = refs
            k_part, v_part = k_ref[:count, :], v_ref[:count, :]
            k_turned = k_part.T
            heads = [(h, slice(s * half, (s + 1) * half)) for h in range(2) for s in range(2)]
            scores = [masked(dot_nt(k_part, q_head[h, at, :]), tail_used) for h, at in heads]
            upstream = [dot_nt(v_part, g_head[h, at, :]) for h, at in heads]
            probs = [jnp.exp(scores[n] - st_ref[n, pl.ds(owner, 1), :]) for n in range(4)]
            dscore = [
                (probs[n] * (upstream[n] - st_ref[n, pl.ds(2 + owner, 1), :])).astype(BF16)
                for n in range(4)
            ]
            low = jnp.concatenate([x.astype(BF16) for x in probs], axis=1)
            dv_part = dot_nn(low, g_head[...].reshape(2 * rows, LANES))
            dk_part = dot_nn(jnp.concatenate(dscore, axis=1), q_head[...].reshape(2 * rows, LANES))
            for h in range(2):
                own = slice(h * HDIM, (h + 1) * HDIM)
                both = jnp.concatenate(dscore[2 * h:2 * h + 2], axis=1)
                turned[p, own, :] = dot_nn(k_turned[own, :], both)
            for ref, part in ((dk_ref, dk_part), (dv_ref, dv_part)):
                ref[:count, :] = part.astype(BF16)
                unused = ref.shape[0] - count
                if unused:
                    ref[count:, :] = jnp.zeros((unused, LANES), BF16)

        by_length(info[3 + p], step)

    first = pl.ds(pl.multiple_of(info[1] * rows, rows), rows)
    other = pl.ds(pl.multiple_of((1 - info[1]) * rows, rows), rows)
    same = info[1] == info[2]

    @pl.when(same)
    def _():
        dq_ref[first, :] = (turned[0] + turned[1]).astype(BF16).T
        dq_ref[other, :] = jnp.zeros((rows, LANES), BF16)

    @pl.when(jnp.logical_not(same))
    def _():
        dq_ref[first, :] = turned[0].astype(BF16).T
        dq_ref[other, :] = turned[1].astype(BF16).T


PARTS = 2


def blocks(slots, pairs, shape, part):
    span, steps = LANES, pairs
    first = part * (steps // PARTS)
    own = pl.BlockSpec((slots, span), lambda i, info: (0, info[0] * steps + first + i))
    sib = pl.BlockSpec((slots, span), lambda i, info: (0, first + i))
    q_block, g_block = (
        pl.BlockSpec(shape[:3] + (1, shape[4], span), lambda i, info, t=t: (0, 0, 0, t, 0, i))
        for t in range(2)
    )
    return own, [own, sib, own, sib, q_block, g_block], first, steps // PARTS


def sizes(operands):
    slots, half = operands[2].shape
    shape = operands[5].shape
    all_rows = shape[0] * shape[1] * shape[2] * shape[4]
    return slots, half, half // LANES, all_rows, all_rows // QRY


LIMIT = pltpu.CompilerParams(
    dimension_semantics=("arbitrary",), vmem_limit_bytes=48 * 1024 * 1024
)


def row_stats(operands, part, begun):
    slots, half, pairs, all_rows, rows = sizes(operands)
    own, in_blocks, first, steps = blocks(slots, pairs, operands[5].shape, part)
    return pl.pallas_call(
        functools.partial(stats_kernel, part == 0),
        grid_spec=pltpu.PrefetchScalarGridSpec(
            num_scalar_prefetch=1,
            grid=(steps,),
            in_specs=in_blocks + [pl.BlockSpec(memory_space=pl.ANY)] * len(begun),
            out_specs=pl.BlockSpec(
                (4, 8, rows // 2), lambda i, info: (first + i, 0, 0)
            ),
            scratch_shapes=[pltpu.VMEM((2, rows, LANES), BF16)] * 2,
        ),
        out_shape=jax.ShapeDtypeStruct((4 * pairs, 8, rows // 2), F32),
        input_output_aliases={7: 0} if begun else {},
        compiler_params=LIMIT,
        cost_estimate=pl.CostEstimate(
            flops=4 * slots * rows * half, bytes_accessed=5 << 20,
            transcendentals=slots * rows * half // HDIM,
        ),
        name="row_stats",
    )(*operands, *begun)


def merge_stats(stats):
    return pl.pallas_call(
        merge_kernel,
        out_shape=jax.ShapeDtypeStruct(stats.shape, F32),
        in_specs=[pl.BlockSpec(memory_space=pltpu.VMEM)],
        out_specs=pl.BlockSpec(memory_space=pltpu.VMEM),
        name="merge_stats",
    )(stats)


def gradients(operands, stats, part, begun):
    slots, half, pairs, all_rows, rows = sizes(operands)
    own, in_blocks, first, steps = blocks(slots, pairs, operands[5].shape, part)
    span = LANES
    sib = pl.BlockSpec((slots, span), lambda i, info: (0, i))
    stat = pl.BlockSpec((4, 8, rows // 2), lambda i, info: (first + i, 0, 0))
    whole = jax.ShapeDtypeStruct((slots, 2 * half), BF16)
    half_part = jax.ShapeDtypeStruct((slots, steps * span), BF16)
    return pl.pallas_call(
        functools.partial(grads_kernel, part == 0),
        grid_spec=pltpu.PrefetchScalarGridSpec(
            num_scalar_prefetch=1,
            grid=(steps,),
            in_specs=in_blocks + [stat] + [pl.BlockSpec(memory_space=pl.ANY)] * len(begun),
            out_specs=[own, sib, own, sib, pl.BlockSpec((all_rows, span), lambda i, info: (0, i))],
            scratch_shapes=[pltpu.VMEM((2, rows, LANES), BF16)] * 2
            + [pltpu.VMEM((2, LANES, rows), F32)],
        ),
        out_shape=[whole, half_part, whole, half_part,
                   jax.ShapeDtypeStruct((all_rows, steps * span), BF16)],
        input_output_aliases={8: 0, 9: 2} if begun else {},
        compiler_params=LIMIT,
        cost_estimate=pl.CostEstimate(
            flops=10 * slots * rows * half, bytes_accessed=8 << 20,
            transcendentals=slots * rows * half // HDIM,
        ),
        name="gradients",
    )(*operands, stats, *begun)


def per_device(x_size, z_size, queries, keys, values, grad_out, lengths, slot_query):
    chips = x_size * z_size
    core = lax.axis_index("core")
    width = keys.shape[2]
    half = width // 2
    span = half // PARTS
    keys, values = keys[0], values[0]

    mine = jnp.concatenate([slot_query, lengths])
    theirs = swap_cores(mine)
    info = jnp.stack([core, mine[0], theirs[0], mine[1], theirs[1]]).astype(jnp.int32)

    def features(value, at, count):
        return lax.dynamic_slice_in_dim(value, at, count, value.ndim - 1)

    both = lax.all_gather(jnp.stack([queries, grad_out]), "core", axis=0, tiled=False)
    own = [
        lax.dynamic_slice_in_dim(both, core * half + part * span, span, 3) for part in range(PARTS)
    ]
    gathered = (
        gather_x_then_z(own[0], x_size),
        gather_z_then_x(own[1], x_size, z_size),
    )
    sib_k = swap_cores(features(keys, (1 - core) * half, half))
    sib_v = swap_cores(features(values, (1 - core) * half, half))
    operands = [(info, keys, sib_k, values, sib_v, rows, rows) for rows in gathered]
    all_rows = sizes(operands[0])[3]

    stats = []
    for part in range(PARTS):
        stats = [row_stats(operands[part], part, stats)]
    stats = lax.all_to_all(stats[0], CHIP, 0, 0, tiled=True)
    stats = lax.all_to_all(merge_stats(stats), CHIP, 0, 0, tiled=True)

    held = all_rows // chips
    own_rows = held // 2
    begun, sibs, sums = [], [], []
    for part in range(PARTS):
        own_dk, sib_dk, own_dv, sib_dv, dq = gradients(operands[part], stats, part, begun)
        begun = [own_dk, own_dv]
        sibs.append((swap_cores(sib_dk), swap_cores(sib_dv)))
        terms = lax.all_to_all(dq.reshape(chips, held, span), CHIP, 0, 0, tiled=True)
        sums.append(jnp.sum(terms.astype(F32), axis=0).astype(BF16))

    own_dk, own_dv = begun
    for part, (sib_dk, sib_dv) in enumerate(sibs):
        at = (1 - core) * half + part * span
        own_dk = lax.dynamic_update_slice_in_dim(own_dk, sib_dk, at, 1)
        own_dv = lax.dynamic_update_slice_in_dim(own_dv, sib_dv, at, 1)

    summed = jnp.concatenate(sums, axis=1)
    kept = lax.dynamic_slice_in_dim(summed, core * own_rows, own_rows, 0)
    given = swap_cores(lax.dynamic_slice_in_dim(summed, (1 - core) * own_rows, own_rows, 0))
    grad_queries = jnp.where(
        core == 0, jnp.concatenate([kept, given], 1), jnp.concatenate([given, kept], 1)
    )
    return grad_queries, own_dk[None], own_dv[None]


def solution(mesh):
    groups = mesh.devices.shape[0]
    x_size, z_size = 4, 8
    fine = Mesh(
        mesh.devices.reshape(groups, x_size, z_size, 2), ("group", "x", "z", "core")
    )
    at = ("group", "x", "z", "core")
    return jax.shard_map(
        functools.partial(per_device, x_size, z_size),
        mesh=fine,
        in_specs=(P(at, None), P(at, None, None), P(at, None, None), P(at, None), P(at), P(at)),
        out_specs=(P(at, None), P(at, None, None), P(at, None, None)),
        check_vma=False,
    )
```

```python
import functools

import jax
import jax.numpy as jnp
from jax import lax
from jax.experimental import pallas as pl
from jax.experimental.pallas import tpu as pltpu
from jax.sharding import Mesh
from jax.sharding import PartitionSpec as P

HDIM = 64
BKT = 64
QRY = 2
LANES = 128
F32 = jnp.float32
BF16 = jnp.bfloat16
CHIP = ("x", "z")


def swap_cores(value):
    return lax.ppermute(value, "core", [(0, 1), (1, 0)])


def repeated(value, count):
    return jnp.broadcast_to(value[None], (count,) + value.shape)


def gather_x_then_z(value, x_size):
    columns = lax.all_to_all(repeated(value, x_size), "x", 0, 0, tiled=True)
    return lax.all_gather(columns, "z", axis=0, tiled=False)


def gather_z_then_x(value, x_size, z_size):
    column = lax.all_to_all(repeated(value, z_size), "z", 0, 0, tiled=True)
    return lax.all_to_all(repeated(column, x_size), "x", 0, 0, tiled=True)


def dot_nt(a, b):
    return lax.dot_general(a, b, (((1,), (1,)), ((), ())), preferred_element_type=F32)


def dot_nn(a, b):
    return lax.dot_general(a, b, (((1,), (0,)), ((), ())), preferred_element_type=F32)


def by_length(buckets, step):
    for most in range(2, 9, 2):

        @pl.when((buckets == most) | (buckets == most - 1))
        def _():
            step(most * BKT, buckets == most)


def masked(scores, tail_used):
    cut = scores.shape[0] - BKT
    tail = jnp.where(tail_used, scores[cut:], -jnp.inf)
    return jnp.concatenate([scores[:cut], tail], axis=0)


def load_rows(z_first, owner, q_ref, g_ref, q_head, g_head):
    z_size, x_size = q_ref.shape[:2] if z_first else q_ref.shape[1::-1]
    column = z_size * q_ref.shape[2] * q_ref.shape[4]
    lane = lax.broadcasted_iota(jnp.int32, (column, LANES), 1)
    for i in range(x_size // QRY):
        x = owner * (x_size // QRY) + i
        at = slice(i * column, (i + 1) * column)
        for ref, head in ((q_ref, q_head), (g_ref, g_head)):
            value = (ref[:, x, :, 0] if z_first else ref[x, :, :, 0]).reshape(column, LANES)
            for h in range(2):
                mine = (lane < HDIM) if h == 0 else (lane >= HDIM)
                head[h, at, :] = jnp.where(mine, value, jnp.zeros_like(value))


def with_rows(p, z_first, info, q_ref, g_ref, q_head, g_head):
    @pl.when((p == 0) | (info[1] != info[2]))
    def _():
        load_rows(z_first, info[1 + p], q_ref, g_ref, q_head, g_head)


def stats_kernel(z_first, info, own_k, sib_k, own_v, sib_v, q_ref, g_ref, *rest):
    out_ref, q_head, g_head = rest[-3:]
    rows = q_head.shape[1]
    half = rows // 2

    for p, (k_ref, v_ref) in enumerate(((own_k, own_v), (sib_k, sib_v))):
        with_rows(p, z_first, info, q_ref, g_ref, q_head, g_head)

        def step(count, tail_used, p=p, k_ref=k_ref, v_ref=v_ref):
            k_part, v_part = k_ref[:count, :], v_ref[:count, :]
            heads = [(h, slice(s * half, (s + 1) * half)) for h in range(2) for s in range(2)]
            scores = [masked(dot_nt(k_part, q_head[h, at, :]), tail_used) for h, at in heads]
            upstream = [dot_nt(v_part, g_head[h, at, :]) for h, at in heads]
            for n in range(4):
                peak = jnp.max(scores[n], axis=0, keepdims=True)
                weights = jnp.exp(scores[n] - peak)
                stats = (
                    peak,
                    jnp.sum(weights, axis=0, keepdims=True),
                    jnp.sum(weights * upstream[n], axis=0, keepdims=True),
                    jnp.full((1, half), info[1 + p].astype(F32)),
                )
                for t, stat in enumerate(stats):
                    out_ref[n, 2 * t + p:2 * t + p + 1, :] = stat

        by_length(info[3 + p], step)


def merge_kernel(in_ref, out_ref):
    chips = in_ref.shape[0]
    merged = []
    tops = [in_ref[:, t, :] for t in range(2)]
    sums = [in_ref[:, 2 + t, :] for t in range(2)]
    dots = [in_ref[:, 4 + t, :] for t in range(2)]
    owners = [in_ref[:, 6 + t, :] for t in range(2)]
    for query in range(QRY):
        held = [jnp.where(owners[t] == query, tops[t], -jnp.inf) for t in range(2)]
        peak = jnp.max(jnp.maximum(held[0], held[1]), axis=0, keepdims=True)
        factors = [jnp.exp(held[t] - peak) for t in range(2)]
        total = jnp.sum(sums[0] * factors[0] + sums[1] * factors[1], axis=0, keepdims=True)
        dotted = jnp.sum(dots[0] * factors[0] + dots[1] * factors[1], axis=0, keepdims=True)
        merged.append((peak + jnp.log(total), dotted / total))
    table = jnp.concatenate(
        [merged[0][0], merged[1][0], merged[0][1], merged[1][1]]
        + [jnp.zeros_like(merged[0][0])] * 4, axis=0
    )
    out_ref[...] = jnp.broadcast_to(table[None], out_ref.shape)


def query_terms(p, turned, k_part, dscore):
    k_turned = k_part.T
    for h in range(2):
        own = slice(h * HDIM, (h + 1) * HDIM)
        both = jnp.concatenate(dscore[2 * h:2 * h + 2], axis=1)
        turned[p, own, :] = dot_nn(k_turned[own, :], both)


def write_query_terms(info, turned, dq_ref):
    rows = turned.shape[2]
    first = pl.ds(pl.multiple_of(info[1] * rows, rows), rows)
    other = pl.ds(pl.multiple_of((1 - info[1]) * rows, rows), rows)
    same = info[1] == info[2]

    @pl.when(same)
    def _():
        dq_ref[first, :] = (turned[0] + turned[1]).astype(BF16).T
        dq_ref[other, :] = jnp.zeros((rows, LANES), BF16)

    @pl.when(jnp.logical_not(same))
    def _():
        dq_ref[first, :] = turned[0].astype(BF16).T
        dq_ref[other, :] = turned[1].astype(BF16).T


def key_terms(probs, dscore, q_head, g_head, dk_ref, dv_ref):
    rows = q_head.shape[1]
    count = probs[0].shape[0]
    low = jnp.concatenate([x.astype(BF16) for x in probs], axis=1)
    dv_part = dot_nn(low, g_head[...].reshape(2 * rows, LANES))
    dk_part = dot_nn(jnp.concatenate(dscore, axis=1), q_head[...].reshape(2 * rows, LANES))
    for ref, part in ((dk_ref, dk_part), (dv_ref, dv_part)):
        ref[:count, :] = part.astype(BF16)
        unused = ref.shape[0] - count
        if unused:
            ref[count:, :] = jnp.zeros((unused, LANES), BF16)


def scored(z_first, p, info, refs, q_ref, g_ref, st_ref, q_head, g_head, use):
    half = q_head.shape[1] // 2
    with_rows(p, z_first, info, q_ref, g_ref, q_head, g_head)
    k_ref, v_ref = refs
    owner = info[1 + p]

    def stat(n, row):
        return st_ref[n, pl.ds(row, 1), :]

    def step(count, tail_used):
        k_part, v_part = k_ref[:count, :], v_ref[:count, :]
        heads = [(h, slice(s * half, (s + 1) * half)) for h in range(2) for s in range(2)]
        scores = [masked(dot_nt(k_part, q_head[h, at, :]), tail_used) for h, at in heads]
        upstream = [dot_nt(v_part, g_head[h, at, :]) for h, at in heads]
        probs = [jnp.exp(scores[n] - stat(n, owner)) for n in range(4)]
        dscore = [(probs[n] * (upstream[n] - stat(n, 2 + owner))).astype(BF16) for n in range(4)]
        use(k_part, probs, dscore)

    by_length(info[3 + p], step)


def dq_kernel(z_first, info, own_k, sib_k, own_v, sib_v, q_ref, g_ref, st_ref, dq_ref,
              q_head, g_head, turned):
    for p, refs in enumerate(((own_k, own_v), (sib_k, sib_v))):

        def use(k_part, probs, dscore, p=p):
            query_terms(p, turned, k_part, dscore)

        scored(z_first, p, info, refs, q_ref, g_ref, st_ref, q_head, g_head, use)

    write_query_terms(info, turned, dq_ref)


def dkv_kernel(z_first, info, own_k, sib_k, own_v, sib_v, q_ref, g_ref, st_ref, *rest):
    own_dk, sib_dk, own_dv, sib_dv, q_head, g_head = rest[-6:]
    sides = ((own_k, own_v, own_dk, own_dv), (sib_k, sib_v, sib_dk, sib_dv))
    for p, (k_ref, v_ref, dk_ref, dv_ref) in enumerate(sides):

        def use(k_part, probs, dscore, dk_ref=dk_ref, dv_ref=dv_ref):
            key_terms(probs, dscore, q_head, g_head, dk_ref, dv_ref)

        scored(z_first, p, info, (k_ref, v_ref), q_ref, g_ref, st_ref, q_head, g_head, use)


def grads_kernel(z_first, info, own_k, sib_k, own_v, sib_v, q_ref, g_ref, st_ref,
                 own_dk, sib_dk, own_dv, sib_dv, dq_ref, q_head, g_head, turned):
    sides = ((own_k, own_v, own_dk, own_dv), (sib_k, sib_v, sib_dk, sib_dv))
    for p, (k_ref, v_ref, dk_ref, dv_ref) in enumerate(sides):

        def use(k_part, probs, dscore, p=p, dk_ref=dk_ref, dv_ref=dv_ref):
            key_terms(probs, dscore, q_head, g_head, dk_ref, dv_ref)
            query_terms(p, turned, k_part, dscore)

        scored(z_first, p, info, (k_ref, v_ref), q_ref, g_ref, st_ref, q_head, g_head, use)

    write_query_terms(info, turned, dq_ref)


def complete_kernel(half, info, *refs):
    sibs, (own_dk, own_dv, held, sems) = refs[:4], refs[-4:]
    span = half // PARTS
    loads, stores = [], []
    for n, sib in enumerate(sibs):
        part, own = n // 2, (own_dk, own_dv)[n % 2]
        at = pl.multiple_of((1 - info[0]) * half + part * span, span)
        loads.append(pltpu.make_async_copy(sib, held.at[n], sems.at[0, n]))
        stores.append(pltpu.make_async_copy(held.at[n], own.at[:, pl.ds(at, span)], sems.at[1, n]))
    for load in loads:
        load.start()
    for load, store in zip(loads, stores):
        load.wait()
        store.start()
    for store in stores:
        store.wait()


PARTS = 2


def blocks(slots, pairs, shape, part):
    span, steps = LANES, pairs
    first = part * (steps // PARTS)
    own = pl.BlockSpec((slots, span), lambda i, info: (0, info[0] * steps + first + i))
    sib = pl.BlockSpec((slots, span), lambda i, info: (0, first + i))
    q_block, g_block = (
        pl.BlockSpec(shape[:3] + (1, shape[4], span), lambda i, info, t=t: (0, 0, 0, t, 0, i))
        for t in range(2)
    )
    return own, [own, sib, own, sib, q_block, g_block], first, steps // PARTS


def sizes(operands):
    slots, half = operands[2].shape
    shape = operands[5].shape
    all_rows = shape[0] * shape[1] * shape[2] * shape[4]
    return slots, half, half // LANES, all_rows, all_rows // QRY


LIMIT = pltpu.CompilerParams(
    dimension_semantics=("arbitrary",), vmem_limit_bytes=48 * 1024 * 1024
)


def row_stats(operands, part, begun):
    slots, half, pairs, all_rows, rows = sizes(operands)
    own, in_blocks, first, steps = blocks(slots, pairs, operands[5].shape, part)
    return pl.pallas_call(
        functools.partial(stats_kernel, part == 0),
        grid_spec=pltpu.PrefetchScalarGridSpec(
            num_scalar_prefetch=1,
            grid=(steps,),
            in_specs=in_blocks + [pl.BlockSpec(memory_space=pl.ANY)] * len(begun),
            out_specs=pl.BlockSpec(
                (4, 8, rows // 2), lambda i, info: (first + i, 0, 0)
            ),
            scratch_shapes=[pltpu.VMEM((2, rows, LANES), BF16)] * 2,
        ),
        out_shape=jax.ShapeDtypeStruct((4 * pairs, 8, rows // 2), F32),
        input_output_aliases={7: 0} if begun else {},
        compiler_params=LIMIT,
        cost_estimate=pl.CostEstimate(
            flops=4 * slots * rows * half, bytes_accessed=5 << 20,
            transcendentals=slots * rows * half // HDIM,
        ),
        name="row_stats",
    )(*operands, *begun)


def merge_stats(stats):
    return pl.pallas_call(
        merge_kernel,
        out_shape=jax.ShapeDtypeStruct(stats.shape, F32),
        in_specs=[pl.BlockSpec(memory_space=pltpu.VMEM)],
        out_specs=pl.BlockSpec(memory_space=pltpu.VMEM),
        name="merge_stats",
    )(stats)


def key_specs(operands, part):
    slots, half, pairs, all_rows, rows = sizes(operands)
    own = blocks(slots, pairs, operands[5].shape, part)[0]
    sib = pl.BlockSpec((slots, LANES), lambda i, info: (0, i))
    whole = jax.ShapeDtypeStruct((slots, 2 * half), BF16)
    half_part = jax.ShapeDtypeStruct((slots, half // PARTS), BF16)
    return [own, sib, own, sib], [whole, half_part, whole, half_part]


def query_specs(operands):
    slots, half, pairs, all_rows, rows = sizes(operands)
    spec = pl.BlockSpec((all_rows, LANES), lambda i, info: (0, i))
    scratch = pltpu.VMEM((2, LANES, rows), F32)
    return [spec], [jax.ShapeDtypeStruct((all_rows, half // PARTS), BF16)], [scratch]


def call(kernel, operands, stats, part, out_specs, out_shape, scratch, begun, share, name):
    slots, half, pairs, all_rows, rows = sizes(operands)
    own, in_blocks, first, steps = blocks(slots, pairs, operands[5].shape, part)
    stat = pl.BlockSpec((4, 8, rows // 2), lambda i, info: (first + i, 0, 0))
    return pl.pallas_call(
        functools.partial(kernel, part == 0),
        grid_spec=pltpu.PrefetchScalarGridSpec(
            num_scalar_prefetch=1,
            grid=(steps,),
            in_specs=in_blocks + [stat] + [pl.BlockSpec(memory_space=pl.ANY)] * len(begun),
            out_specs=out_specs,
            scratch_shapes=[pltpu.VMEM((2, rows, LANES), BF16)] * 2 + scratch,
        ),
        out_shape=out_shape,
        input_output_aliases={8: 0, 9: 2} if begun else {},
        compiler_params=LIMIT,
        cost_estimate=pl.CostEstimate(
            flops=share * slots * rows * half, bytes_accessed=share << 20,
            transcendentals=slots * rows * half // HDIM,
        ),
        name=name,
    )(*operands, stats, *begun)


def query_gradients(operands, stats, part):
    specs, shapes, scratch = query_specs(operands)
    return call(
        dq_kernel, operands, stats, part, specs, shapes, scratch, [], 6, "query_gradients"
    )[0]


def key_gradients(operands, stats, part, begun):
    specs, shapes = key_specs(operands, part)
    return call(dkv_kernel, operands, stats, part, specs, shapes, [], begun, 8, "key_gradients")


def gradients(operands, stats, part):
    specs, shapes = key_specs(operands, part)
    more_specs, more_shapes, scratch = query_specs(operands)
    return call(
        grads_kernel, operands, stats, part, specs + more_specs, shapes + more_shapes, scratch,
        [], 10, "gradients",
    )


def completed(info, sibs, own_dk, own_dv):
    anywhere = pl.BlockSpec(memory_space=pl.ANY)
    shape = jax.ShapeDtypeStruct(own_dk.shape, BF16)
    return pl.pallas_call(
        functools.partial(complete_kernel, own_dk.shape[1] // 2),
        grid_spec=pltpu.PrefetchScalarGridSpec(
            num_scalar_prefetch=1,
            grid=(1,),
            in_specs=[anywhere] * 6,
            out_specs=[anywhere] * 2,
            scratch_shapes=[
                pltpu.VMEM((4,) + sibs[0].shape, BF16), pltpu.SemaphoreType.DMA((2, 4))
            ],
        ),
        out_shape=[shape, shape],
        input_output_aliases={5: 0, 6: 1},
        cost_estimate=pl.CostEstimate(flops=0, bytes_accessed=8 << 20, transcendentals=0),
        name="complete_keys",
    )(info, *sibs, own_dk, own_dv)


def per_device(x_size, z_size, queries, keys, values, grad_out, lengths, slot_query):
    chips = x_size * z_size
    core = lax.axis_index("core")
    width = keys.shape[2]
    half = width // 2
    span = half // PARTS
    keys, values = keys[0], values[0]

    mine = jnp.concatenate([slot_query, lengths])
    theirs = swap_cores(mine)
    info = jnp.stack([core, mine[0], theirs[0], mine[1], theirs[1]]).astype(jnp.int32)

    def features(value, at, count):
        return lax.dynamic_slice_in_dim(value, at, count, value.ndim - 1)

    both = lax.all_gather(jnp.stack([queries, grad_out]), "core", axis=0, tiled=False)
    own = [
        lax.dynamic_slice_in_dim(both, core * half + part * span, span, 3) for part in range(PARTS)
    ]
    gathered = (
        gather_x_then_z(own[0], x_size),
        gather_z_then_x(own[1], x_size, z_size),
    )
    sib_k = swap_cores(features(keys, (1 - core) * half, half))
    sib_v = swap_cores(features(values, (1 - core) * half, half))
    operands = [(info, keys, sib_k, values, sib_v, rows, rows) for rows in gathered]
    all_rows = sizes(operands[0])[3]

    stats = []
    for part in range(PARTS):
        stats = [row_stats(operands[part], part, stats)]
    stats = lax.all_to_all(stats[0], CHIP, 0, 0, tiled=True)
    stats = lax.all_to_all(merge_stats(stats), CHIP, 0, 0, tiled=True)

    held = all_rows // chips
    own_rows = held // 2

    def to_owners(dq):
        return lax.all_to_all(dq.reshape(chips, held, span), CHIP, 0, 0, tiled=True)

    first_terms = to_owners(query_gradients(operands[0], stats, 0))
    own_dk, sib_dk_1, own_dv, sib_dv_1, dq = gradients(operands[1], stats, 1)
    second_terms = to_owners(dq)
    sibs = [swap_cores(sib_dk_1), swap_cores(sib_dv_1)]
    stats, first_terms = lax.optimization_barrier((stats, first_terms))
    own_dk, sib_dk_0, own_dv, sib_dv_0 = key_gradients(operands[0], stats, 0, [own_dk, own_dv])
    sibs = [swap_cores(sib_dk_0), swap_cores(sib_dv_0)] + sibs
    own_dk, own_dv = completed(info, sibs, own_dk, own_dv)
    own_dk, second_terms = lax.optimization_barrier((own_dk, second_terms))
    sums = [
        jnp.sum(terms.astype(F32), axis=0).astype(BF16) for terms in (first_terms, second_terms)
    ]

    summed = jnp.concatenate(sums, axis=1)
    kept = lax.dynamic_slice_in_dim(summed, core * own_rows, own_rows, 0)
    given = swap_cores(lax.dynamic_slice_in_dim(summed, (1 - core) * own_rows, own_rows, 0))
    grad_queries = jnp.where(
        core == 0, jnp.concatenate([kept, given], 1), jnp.concatenate([given, kept], 1)
    )
    return grad_queries, own_dk[None], own_dv[None]


def solution(mesh):
    groups = mesh.devices.shape[0]
    x_size, z_size = 4, 8
    fine = Mesh(
        mesh.devices.reshape(groups, x_size, z_size, 2), ("group", "x", "z", "core")
    )
    at = ("group", "x", "z", "core")
    return jax.shard_map(
        functools.partial(per_device, x_size, z_size),
        mesh=fine,
        in_specs=(P(at, None), P(at, None, None), P(at, None, None), P(at, None), P(at), P(at)),
        out_specs=(P(at, None), P(at, None, None), P(at, None, None)),
        check_vma=False,
    )
```

```python
import functools

import jax
import jax.numpy as jnp
from jax import lax
from jax.experimental import pallas as pl
from jax.experimental.pallas import tpu as pltpu
from jax.sharding import Mesh
from jax.sharding import PartitionSpec as P

HDIM = 64
BKT = 64
QRY = 2
LANES = 128
F32 = jnp.float32
BF16 = jnp.bfloat16
CHIP = ("x", "z")


def swap_cores(value):
    return lax.ppermute(value, "core", [(0, 1), (1, 0)])


def repeated(value, count):
    return jnp.broadcast_to(value[None], (count,) + value.shape)


def gather_x_then_z(value, x_size):
    columns = lax.all_to_all(repeated(value, x_size), "x", 0, 0, tiled=True)
    return lax.all_gather(columns, "z", axis=0, tiled=False)


def gather_z_then_x(value, x_size, z_size):
    column = lax.all_to_all(repeated(value, z_size), "z", 0, 0, tiled=True)
    return lax.all_to_all(repeated(column, x_size), "x", 0, 0, tiled=True)


def dot_nt(a, b):
    return lax.dot_general(a, b, (((1,), (1,)), ((), ())), preferred_element_type=F32)


def dot_nn(a, b):
    return lax.dot_general(a, b, (((1,), (0,)), ((), ())), preferred_element_type=F32)


def by_length(buckets, step):
    for most in range(2, 9, 2):

        @pl.when((buckets == most) | (buckets == most - 1))
        def _():
            step(most * BKT, buckets == most)


def masked(scores, tail_used):
    cut = scores.shape[0] - BKT
    tail = jnp.where(tail_used, scores[cut:], -jnp.inf)
    return jnp.concatenate([scores[:cut], tail], axis=0)


def load_rows(z_first, owner, q_ref, g_ref, q_head, g_head):
    z_size, x_size = q_ref.shape[:2] if z_first else q_ref.shape[1::-1]
    column = z_size * q_ref.shape[2] * q_ref.shape[4]
    lane = lax.broadcasted_iota(jnp.int32, (column, LANES), 1)
    for i in range(x_size // QRY):
        x = owner * (x_size // QRY) + i
        at = slice(i * column, (i + 1) * column)
        for ref, head in ((q_ref, q_head), (g_ref, g_head)):
            value = (ref[:, x, :, 0] if z_first else ref[x, :, :, 0]).reshape(column, LANES)
            for h in range(2):
                mine = (lane < HDIM) if h == 0 else (lane >= HDIM)
                head[h, at, :] = jnp.where(mine, value, jnp.zeros_like(value))


def with_rows(p, z_first, info, q_ref, g_ref, q_head, g_head):
    @pl.when((p == 0) | (info[1] != info[2]))
    def _():
        load_rows(z_first, info[1 + p], q_ref, g_ref, q_head, g_head)


def stats_kernel(z_first, info, own_k, sib_k, own_v, sib_v, q_ref, g_ref, *rest):
    out_ref, q_head, g_head, held = rest[-4:]
    rows = q_head.shape[1]
    half = rows // 2

    for p, (k_ref, v_ref) in enumerate(((own_k, own_v), (sib_k, sib_v))):
        with_rows(p, z_first, info, q_ref, g_ref, q_head, g_head)

        def step(count, tail_used, p=p, k_ref=k_ref, v_ref=v_ref):
            k_part, v_part = k_ref[:count, :], v_ref[:count, :]
            heads = [(h, slice(s * half, (s + 1) * half)) for h in range(2) for s in range(2)]
            scores = [masked(dot_nt(k_part, q_head[h, at, :]), tail_used) for h, at in heads]
            upstream = [dot_nt(v_part, g_head[h, at, :]) for h, at in heads]
            for n in range(4):
                peak = jnp.max(scores[n], axis=0, keepdims=True)
                weights = jnp.exp(scores[n] - peak)
                total = jnp.sum(weights, axis=0, keepdims=True)
                dotted = jnp.sum(weights * upstream[n], axis=0, keepdims=True)
                held[p, 0, n:n + 1, :] = peak + jnp.log(total)
                held[p, 1, n:n + 1, :] = dotted / total

        by_length(info[3 + p], step)

    same = info[1] == info[2]
    first = (held[0, 0], held[0, 1])
    second = (held[1, 0], held[1, 1])

    def write(query, top, delta):
        for n in range(4):
            out_ref[n, pl.ds(query, 1), :] = top[n:n + 1]
            out_ref[n, pl.ds(QRY + query, 1), :] = delta[n:n + 1]

    @pl.when(same)
    def _():
        write(info[1], *joined(jnp.stack([first[0], second[0]]), jnp.stack([first[1], second[1]])))
        write(1 - info[1], jnp.full_like(first[0], -jnp.inf), jnp.zeros_like(first[1]))

    @pl.when(jnp.logical_not(same))
    def _():
        write(info[1], *first)
        write(info[2], *second)


def joined(tops, deltas):
    peak = jnp.max(tops, axis=0)
    factors = jnp.exp(tops - peak[None])
    total = jnp.sum(factors, axis=0)
    return peak + jnp.log(total), jnp.sum(deltas * factors, axis=0) / total


def merge_kernel(in_ref, out_ref):
    table = in_ref[...]
    tops, deltas = joined(table[:, :QRY], table[:, QRY:])
    out_ref[...] = jnp.broadcast_to(jnp.concatenate([tops, deltas])[None], out_ref.shape)


def query_terms(p, turned, k_part, dscore):
    k_turned = k_part.T
    for h in range(2):
        own = slice(h * HDIM, (h + 1) * HDIM)
        both = jnp.concatenate(dscore[2 * h:2 * h + 2], axis=1)
        turned[p, own, :] = dot_nn(k_turned[own, :], both)


def write_query_terms(info, turned, dq_ref):
    rows = turned.shape[2]
    first = pl.ds(pl.multiple_of(info[1] * rows, rows), rows)
    other = pl.ds(pl.multiple_of((1 - info[1]) * rows, rows), rows)
    same = info[1] == info[2]

    @pl.when(same)
    def _():
        dq_ref[first, :] = (turned[0] + turned[1]).astype(BF16).T
        dq_ref[other, :] = jnp.zeros((rows, LANES), BF16)

    @pl.when(jnp.logical_not(same))
    def _():
        dq_ref[first, :] = turned[0].astype(BF16).T
        dq_ref[other, :] = turned[1].astype(BF16).T


def key_terms(probs, dscore, q_head, g_head, dk_ref, dv_ref):
    rows = q_head.shape[1]
    count = probs[0].shape[0]
    low = jnp.concatenate([x.astype(BF16) for x in probs], axis=1)
    dv_part = dot_nn(low, g_head[...].reshape(2 * rows, LANES))
    dk_part = dot_nn(jnp.concatenate(dscore, axis=1), q_head[...].reshape(2 * rows, LANES))
    for ref, part in ((dk_ref, dk_part), (dv_ref, dv_part)):
        ref[:count, :] = part.astype(BF16)
        unused = ref.shape[0] - count
        if unused:
            ref[count:, :] = jnp.zeros((unused, LANES), BF16)


def scored(z_first, p, info, refs, q_ref, g_ref, st_ref, q_head, g_head, use):
    half = q_head.shape[1] // 2
    with_rows(p, z_first, info, q_ref, g_ref, q_head, g_head)
    k_ref, v_ref = refs
    owner = info[1 + p]

    def stat(n, row):
        return st_ref[n, pl.ds(row, 1), :]

    def step(count, tail_used):
        k_part, v_part = k_ref[:count, :], v_ref[:count, :]
        heads = [(h, slice(s * half, (s + 1) * half)) for h in range(2) for s in range(2)]
        scores = [masked(dot_nt(k_part, q_head[h, at, :]), tail_used) for h, at in heads]
        upstream = [dot_nt(v_part, g_head[h, at, :]) for h, at in heads]
        probs = [jnp.exp(scores[n] - stat(n, owner)) for n in range(4)]
        dscore = [(probs[n] * (upstream[n] - stat(n, 2 + owner))).astype(BF16) for n in range(4)]
        use(k_part, probs, dscore)

    by_length(info[3 + p], step)


def dq_kernel(z_first, info, own_k, sib_k, own_v, sib_v, q_ref, g_ref, st_ref, dq_ref,
              q_head, g_head, turned):
    for p, refs in enumerate(((own_k, own_v), (sib_k, sib_v))):

        def use(k_part, probs, dscore, p=p):
            query_terms(p, turned, k_part, dscore)

        scored(z_first, p, info, refs, q_ref, g_ref, st_ref, q_head, g_head, use)

    write_query_terms(info, turned, dq_ref)


def dkv_kernel(z_first, info, own_k, sib_k, own_v, sib_v, q_ref, g_ref, st_ref, *rest):
    own_dk, sib_dk, own_dv, sib_dv, q_head, g_head = rest[-6:]
    sides = ((own_k, own_v, own_dk, own_dv), (sib_k, sib_v, sib_dk, sib_dv))
    for p, (k_ref, v_ref, dk_ref, dv_ref) in enumerate(sides):

        def use(k_part, probs, dscore, dk_ref=dk_ref, dv_ref=dv_ref):
            key_terms(probs, dscore, q_head, g_head, dk_ref, dv_ref)

        scored(z_first, p, info, (k_ref, v_ref), q_ref, g_ref, st_ref, q_head, g_head, use)


def grads_kernel(z_first, info, own_k, sib_k, own_v, sib_v, q_ref, g_ref, st_ref,
                 own_dk, sib_dk, own_dv, sib_dv, dq_ref, q_head, g_head, turned):
    sides = ((own_k, own_v, own_dk, own_dv), (sib_k, sib_v, sib_dk, sib_dv))
    for p, (k_ref, v_ref, dk_ref, dv_ref) in enumerate(sides):

        def use(k_part, probs, dscore, p=p, dk_ref=dk_ref, dv_ref=dv_ref):
            key_terms(probs, dscore, q_head, g_head, dk_ref, dv_ref)
            query_terms(p, turned, k_part, dscore)

        scored(z_first, p, info, (k_ref, v_ref), q_ref, g_ref, st_ref, q_head, g_head, use)

    write_query_terms(info, turned, dq_ref)


def complete_kernel(half, info, *refs):
    sibs, (own_dk, own_dv, held, sems) = refs[:4], refs[-4:]
    span = half // PARTS
    loads, stores = [], []
    for n, sib in enumerate(sibs):
        part, own = n // 2, (own_dk, own_dv)[n % 2]
        at = pl.multiple_of((1 - info[0]) * half + part * span, span)
        loads.append(pltpu.make_async_copy(sib, held.at[n], sems.at[0, n]))
        stores.append(pltpu.make_async_copy(held.at[n], own.at[:, pl.ds(at, span)], sems.at[1, n]))
    for load in loads:
        load.start()
    for load, store in zip(loads, stores):
        load.wait()
        store.start()
    for store in stores:
        store.wait()


PARTS = 2


def blocks(slots, pairs, shape, part):
    span, steps = LANES, pairs
    first = part * (steps // PARTS)
    own = pl.BlockSpec((slots, span), lambda i, info: (0, info[0] * steps + first + i))
    sib = pl.BlockSpec((slots, span), lambda i, info: (0, first + i))
    q_block, g_block = (
        pl.BlockSpec(shape[:3] + (1, shape[4], span), lambda i, info, t=t: (0, 0, 0, t, 0, i))
        for t in range(2)
    )
    return own, [own, sib, own, sib, q_block, g_block], first, steps // PARTS


def sizes(operands):
    slots, half = operands[2].shape
    shape = operands[5].shape
    all_rows = shape[0] * shape[1] * shape[2] * shape[4]
    return slots, half, half // LANES, all_rows, all_rows // QRY


LIMIT = pltpu.CompilerParams(
    dimension_semantics=("arbitrary",), vmem_limit_bytes=48 * 1024 * 1024
)


def row_stats(operands, part, begun):
    slots, half, pairs, all_rows, rows = sizes(operands)
    own, in_blocks, first, steps = blocks(slots, pairs, operands[5].shape, part)
    return pl.pallas_call(
        functools.partial(stats_kernel, part == 0),
        grid_spec=pltpu.PrefetchScalarGridSpec(
            num_scalar_prefetch=1,
            grid=(steps,),
            in_specs=in_blocks + [pl.BlockSpec(memory_space=pl.ANY)] * len(begun),
            out_specs=pl.BlockSpec(
                (4, 2 * QRY, rows // 2), lambda i, info: (first + i, 0, 0)
            ),
            scratch_shapes=[pltpu.VMEM((2, rows, LANES), BF16)] * 2
            + [pltpu.VMEM((2, 2, 4, rows // 2), F32)],
        ),
        out_shape=jax.ShapeDtypeStruct((4 * pairs, 2 * QRY, rows // 2), F32),
        input_output_aliases={7: 0} if begun else {},
        compiler_params=LIMIT,
        cost_estimate=pl.CostEstimate(
            flops=4 * slots * rows * half, bytes_accessed=5 << 20,
            transcendentals=slots * rows * half // HDIM,
        ),
        name="row_stats",
    )(*operands, *begun)


def merge_stats(stats):
    return pl.pallas_call(
        merge_kernel,
        out_shape=jax.ShapeDtypeStruct(stats.shape, F32),
        in_specs=[pl.BlockSpec(memory_space=pltpu.VMEM)],
        out_specs=pl.BlockSpec(memory_space=pltpu.VMEM),
        name="merge_stats",
    )(stats)


def key_specs(operands, part):
    slots, half, pairs, all_rows, rows = sizes(operands)
    own = blocks(slots, pairs, operands[5].shape, part)[0]
    sib = pl.BlockSpec((slots, LANES), lambda i, info: (0, i))
    whole = jax.ShapeDtypeStruct((slots, 2 * half), BF16)
    half_part = jax.ShapeDtypeStruct((slots, half // PARTS), BF16)
    return [own, sib, own, sib], [whole, half_part, whole, half_part]


def query_specs(operands):
    slots, half, pairs, all_rows, rows = sizes(operands)
    spec = pl.BlockSpec((all_rows, LANES), lambda i, info: (0, i))
    scratch = pltpu.VMEM((2, LANES, rows), F32)
    return [spec], [jax.ShapeDtypeStruct((all_rows, half // PARTS), BF16)], [scratch]


def call(kernel, operands, stats, part, out_specs, out_shape, scratch, begun, share, name):
    slots, half, pairs, all_rows, rows = sizes(operands)
    own, in_blocks, first, steps = blocks(slots, pairs, operands[5].shape, part)
    stat = pl.BlockSpec((4, 2 * QRY, rows // 2), lambda i, info: (first + i, 0, 0))
    return pl.pallas_call(
        functools.partial(kernel, part == 0),
        grid_spec=pltpu.PrefetchScalarGridSpec(
            num_scalar_prefetch=1,
            grid=(steps,),
            in_specs=in_blocks + [stat] + [pl.BlockSpec(memory_space=pl.ANY)] * len(begun),
            out_specs=out_specs,
            scratch_shapes=[pltpu.VMEM((2, rows, LANES), BF16)] * 2 + scratch,
        ),
        out_shape=out_shape,
        input_output_aliases={8: 0, 9: 2} if begun else {},
        compiler_params=LIMIT,
        cost_estimate=pl.CostEstimate(
            flops=share * slots * rows * half, bytes_accessed=share << 20,
            transcendentals=slots * rows * half // HDIM,
        ),
        name=name,
    )(*operands, stats, *begun)


def query_gradients(operands, stats, part):
    specs, shapes, scratch = query_specs(operands)
    return call(
        dq_kernel, operands, stats, part, specs, shapes, scratch, [], 6, "query_gradients"
    )[0]


def key_gradients(operands, stats, part, begun):
    specs, shapes = key_specs(operands, part)
    return call(dkv_kernel, operands, stats, part, specs, shapes, [], begun, 8, "key_gradients")


def gradients(operands, stats, part):
    specs, shapes = key_specs(operands, part)
    more_specs, more_shapes, scratch = query_specs(operands)
    return call(
        grads_kernel, operands, stats, part, specs + more_specs, shapes + more_shapes, scratch,
        [], 10, "gradients",
    )


def completed(info, sibs, own_dk, own_dv):
    anywhere = pl.BlockSpec(memory_space=pl.ANY)
    shape = jax.ShapeDtypeStruct(own_dk.shape, BF16)
    return pl.pallas_call(
        functools.partial(complete_kernel, own_dk.shape[1] // 2),
        grid_spec=pltpu.PrefetchScalarGridSpec(
            num_scalar_prefetch=1,
            grid=(1,),
            in_specs=[anywhere] * 6,
            out_specs=[anywhere] * 2,
            scratch_shapes=[
                pltpu.VMEM((4,) + sibs[0].shape, BF16), pltpu.SemaphoreType.DMA((2, 4))
            ],
        ),
        out_shape=[shape, shape],
        input_output_aliases={5: 0, 6: 1},
        cost_estimate=pl.CostEstimate(flops=0, bytes_accessed=8 << 20, transcendentals=0),
        name="complete_keys",
    )(info, *sibs, own_dk, own_dv)


def per_device(x_size, z_size, queries, keys, values, grad_out, lengths, slot_query):
    chips = x_size * z_size
    core = lax.axis_index("core")
    width = keys.shape[2]
    half = width // 2
    span = half // PARTS
    keys, values = keys[0], values[0]

    mine = jnp.concatenate([slot_query, lengths])
    theirs = swap_cores(mine)
    info = jnp.stack([core, mine[0], theirs[0], mine[1], theirs[1]]).astype(jnp.int32)

    def features(value, at, count):
        return lax.dynamic_slice_in_dim(value, at, count, value.ndim - 1)

    both = lax.all_gather(jnp.stack([queries, grad_out]), "core", axis=0, tiled=False)
    own = [
        lax.dynamic_slice_in_dim(both, core * half + part * span, span, 3) for part in range(PARTS)
    ]
    gathered = (
        gather_x_then_z(own[0], x_size),
        gather_z_then_x(own[1], x_size, z_size),
    )
    sib_k = swap_cores(features(keys, (1 - core) * half, half))
    sib_v = swap_cores(features(values, (1 - core) * half, half))
    operands = [(info, keys, sib_k, values, sib_v, rows, rows) for rows in gathered]
    all_rows = sizes(operands[0])[3]

    stats = []
    for part in range(PARTS):
        stats = [row_stats(operands[part], part, stats)]
    stats = lax.all_to_all(stats[0], CHIP, 0, 0, tiled=True)
    stats = lax.all_to_all(merge_stats(stats), CHIP, 0, 0, tiled=True)

    held = all_rows // chips
    own_rows = held // 2

    def to_owners(dq):
        return lax.all_to_all(dq.reshape(chips, held, span), CHIP, 0, 0, tiled=True)

    first_terms = to_owners(query_gradients(operands[0], stats, 0))
    own_dk, sib_dk_1, own_dv, sib_dv_1, dq = gradients(operands[1], stats, 1)
    second_terms = to_owners(dq)
    sibs = [swap_cores(sib_dk_1), swap_cores(sib_dv_1)]
    stats, first_terms = lax.optimization_barrier((stats, first_terms))
    own_dk, sib_dk_0, own_dv, sib_dv_0 = key_gradients(operands[0], stats, 0, [own_dk, own_dv])
    sibs = [swap_cores(sib_dk_0), swap_cores(sib_dv_0)] + sibs
    own_dk, own_dv = completed(info, sibs, own_dk, own_dv)
    own_dk, second_terms = lax.optimization_barrier((own_dk, second_terms))
    sums = [
        jnp.sum(terms.astype(F32), axis=0).astype(BF16) for terms in (first_terms, second_terms)
    ]

    summed = jnp.concatenate(sums, axis=1)
    kept = lax.dynamic_slice_in_dim(summed, core * own_rows, own_rows, 0)
    given = swap_cores(lax.dynamic_slice_in_dim(summed, (1 - core) * own_rows, own_rows, 0))
    grad_queries = jnp.where(
        core == 0, jnp.concatenate([kept, given], 1), jnp.concatenate([given, kept], 1)
    )
    return grad_queries, own_dk[None], own_dv[None]


def solution(mesh):
    groups = mesh.devices.shape[0]
    x_size, z_size = 4, 8
    fine = Mesh(
        mesh.devices.reshape(groups, x_size, z_size, 2), ("group", "x", "z", "core")
    )
    at = ("group", "x", "z", "core")
    return jax.shard_map(
        functools.partial(per_device, x_size, z_size),
        mesh=fine,
        in_specs=(P(at, None), P(at, None, None), P(at, None, None), P(at, None), P(at), P(at)),
        out_specs=(P(at, None), P(at, None, None), P(at, None, None)),
        check_vma=False,
    )
```

```python
import functools

import jax
import jax.numpy as jnp
from jax import lax
from jax.experimental import pallas as pl
from jax.experimental.pallas import tpu as pltpu
from jax.sharding import Mesh
from jax.sharding import PartitionSpec as P

HDIM = 64
BKT = 64
QRY = 2
LANES = 128
F32 = jnp.float32
BF16 = jnp.bfloat16
CHIP = ("x", "z")


def swap_cores(value):
    return lax.ppermute(value, "core", [(0, 1), (1, 0)])


def repeated(value, count):
    return jnp.broadcast_to(value[None], (count,) + value.shape)


def gather_x_then_z(value, x_size):
    columns = lax.all_to_all(repeated(value, x_size), "x", 0, 0, tiled=True)
    return lax.all_gather(columns, "z", axis=0, tiled=False)


def gather_z_then_x(value, x_size, z_size):
    column = lax.all_to_all(repeated(value, z_size), "z", 0, 0, tiled=True)
    return lax.all_to_all(repeated(column, x_size), "x", 0, 0, tiled=True)


def dot_nt(a, b):
    return lax.dot_general(a, b, (((1,), (1,)), ((), ())), preferred_element_type=F32)


def dot_nn(a, b):
    return lax.dot_general(a, b, (((1,), (0,)), ((), ())), preferred_element_type=F32)


def by_length(buckets, step):
    for most in range(2, 9, 2):

        @pl.when((buckets == most) | (buckets == most - 1))
        def _():
            step(most * BKT, buckets == most)


def masked(scores, tail_used):
    cut = scores.shape[0] - BKT
    tail = jnp.where(tail_used, scores[cut:], -jnp.inf)
    return jnp.concatenate([scores[:cut], tail], axis=0)


def load_rows(z_first, owner, q_ref, g_ref, q_head, g_head):
    z_size, x_size = q_ref.shape[:2] if z_first else q_ref.shape[1::-1]
    column = z_size * q_ref.shape[2] * q_ref.shape[4]
    lane = lax.broadcasted_iota(jnp.int32, (column, LANES), 1)
    for i in range(x_size // QRY):
        x = owner * (x_size // QRY) + i
        at = slice(i * column, (i + 1) * column)
        for ref, head in ((q_ref, q_head), (g_ref, g_head)):
            value = (ref[:, x, :, 0] if z_first else ref[x, :, :, 0]).reshape(column, LANES)
            for h in range(2):
                mine = (lane < HDIM) if h == 0 else (lane >= HDIM)
                head[h, at, :] = jnp.where(mine, value, jnp.zeros_like(value))


def with_rows(p, z_first, info, q_ref, g_ref, q_head, g_head):
    @pl.when((p == 0) | (info[1] != info[2]))
    def _():
        load_rows(z_first, info[1 + p], q_ref, g_ref, q_head, g_head)


def stats_kernel(z_first, info, own_k, sib_k, own_v, sib_v, q_ref, g_ref, *rest):
    out_ref, q_head, g_head, held = rest[-4:]
    rows = q_head.shape[1]
    half = rows // 2

    for p, (k_ref, v_ref) in enumerate(((own_k, own_v), (sib_k, sib_v))):
        with_rows(p, z_first, info, q_ref, g_ref, q_head, g_head)

        def step(count, tail_used, p=p, k_ref=k_ref, v_ref=v_ref):
            k_part, v_part = k_ref[:count, :], v_ref[:count, :]
            heads = [(h, slice(s * half, (s + 1) * half)) for h in range(2) for s in range(2)]
            scores = [masked(dot_nt(k_part, q_head[h, at, :]), tail_used) for h, at in heads]
            upstream = [dot_nt(v_part, g_head[h, at, :]) for h, at in heads]
            for n in range(4):
                peak = jnp.max(scores[n], axis=0, keepdims=True)
                weights = jnp.exp(scores[n] - peak)
                total = jnp.sum(weights, axis=0, keepdims=True)
                dotted = jnp.sum(weights * upstream[n], axis=0, keepdims=True)
                held[p, 0, n:n + 1, :] = peak + jnp.log(total)
                held[p, 1, n:n + 1, :] = dotted / total

        by_length(info[3 + p], step)

    same = info[1] == info[2]
    first = (held[0, 0], held[0, 1])
    second = (held[1, 0], held[1, 1])

    def write(query, top, delta):
        for n in range(4):
            out_ref[n, pl.ds(query, 1), :] = top[n:n + 1]
            out_ref[n, pl.ds(QRY + query, 1), :] = delta[n:n + 1]

    @pl.when(same)
    def _():
        write(info[1], *joined(jnp.stack([first[0], second[0]]), jnp.stack([first[1], second[1]])))
        write(1 - info[1], jnp.full_like(first[0], -jnp.inf), jnp.zeros_like(first[1]))

    @pl.when(jnp.logical_not(same))
    def _():
        write(info[1], *first)
        write(info[2], *second)


def joined(tops, deltas):
    peak = jnp.max(tops, axis=0)
    factors = jnp.exp(tops - peak[None])
    total = jnp.sum(factors, axis=0)
    return peak + jnp.log(total), jnp.sum(deltas * factors, axis=0) / total


def merge_kernel(in_ref, out_ref):
    table = in_ref[...]
    tops, deltas = joined(table[:, :QRY], table[:, QRY:])
    out_ref[...] = jnp.broadcast_to(jnp.concatenate([tops, deltas])[None], out_ref.shape)


def query_terms(p, turned, k_part, dscore):
    k_turned = k_part.T
    for h in range(2):
        own = slice(h * HDIM, (h + 1) * HDIM)
        both = jnp.concatenate(dscore[2 * h:2 * h + 2], axis=1)
        turned[p, own, :] = dot_nn(k_turned[own, :], both)


def write_query_terms(info, turned, dq_ref):
    rows = turned.shape[2]
    first = pl.ds(pl.multiple_of(info[1] * rows, rows), rows)
    other = pl.ds(pl.multiple_of((1 - info[1]) * rows, rows), rows)
    same = info[1] == info[2]

    @pl.when(same)
    def _():
        dq_ref[first, :] = (turned[0] + turned[1]).astype(BF16).T
        dq_ref[other, :] = jnp.zeros((rows, LANES), BF16)

    @pl.when(jnp.logical_not(same))
    def _():
        dq_ref[first, :] = turned[0].astype(BF16).T
        dq_ref[other, :] = turned[1].astype(BF16).T


def key_terms(probs, dscore, q_head, g_head, dk_ref, dv_ref):
    rows = q_head.shape[1]
    count = probs[0].shape[0]
    low = jnp.concatenate([x.astype(BF16) for x in probs], axis=1)
    dv_part = dot_nn(low, g_head[...].reshape(2 * rows, LANES))
    dk_part = dot_nn(jnp.concatenate(dscore, axis=1), q_head[...].reshape(2 * rows, LANES))
    for ref, part in ((dk_ref, dk_part), (dv_ref, dv_part)):
        ref[:count, :] = part.astype(BF16)
        unused = ref.shape[0] - count
        if unused:
            ref[count:, :] = jnp.zeros((unused, LANES), BF16)


def scored(z_first, p, info, refs, q_ref, g_ref, st_ref, q_head, g_head, use):
    half = q_head.shape[1] // 2
    with_rows(p, z_first, info, q_ref, g_ref, q_head, g_head)
    k_ref, v_ref = refs
    owner = info[1 + p]

    def stat(n, row):
        return st_ref[n, pl.ds(row, 1), :]

    def step(count, tail_used):
        k_part, v_part = k_ref[:count, :], v_ref[:count, :]
        heads = [(h, slice(s * half, (s + 1) * half)) for h in range(2) for s in range(2)]
        scores = [masked(dot_nt(k_part, q_head[h, at, :]), tail_used) for h, at in heads]
        upstream = [dot_nt(v_part, g_head[h, at, :]) for h, at in heads]
        probs = [jnp.exp(scores[n] - stat(n, owner)) for n in range(4)]
        dscore = [(probs[n] * (upstream[n] - stat(n, 2 + owner))).astype(BF16) for n in range(4)]
        use(k_part, probs, dscore)

    by_length(info[3 + p], step)


def dq_kernel(z_first, info, own_k, sib_k, own_v, sib_v, q_ref, g_ref, st_ref, dq_ref,
              q_head, g_head, turned):
    for p, refs in enumerate(((own_k, own_v), (sib_k, sib_v))):

        def use(k_part, probs, dscore, p=p):
            query_terms(p, turned, k_part, dscore)

        scored(z_first, p, info, refs, q_ref, g_ref, st_ref, q_head, g_head, use)

    write_query_terms(info, turned, dq_ref)


def dkv_kernel(z_first, info, own_k, sib_k, own_v, sib_v, q_ref, g_ref, st_ref, *rest):
    own_dk, sib_dk, own_dv, sib_dv, q_head, g_head = rest[-6:]
    sides = ((own_k, own_v, own_dk, own_dv), (sib_k, sib_v, sib_dk, sib_dv))
    for p, (k_ref, v_ref, dk_ref, dv_ref) in enumerate(sides):

        def use(k_part, probs, dscore, dk_ref=dk_ref, dv_ref=dv_ref):
            key_terms(probs, dscore, q_head, g_head, dk_ref, dv_ref)

        scored(z_first, p, info, (k_ref, v_ref), q_ref, g_ref, st_ref, q_head, g_head, use)


def grads_kernel(z_first, info, own_k, sib_k, own_v, sib_v, q_ref, g_ref, st_ref,
                 own_dk, sib_dk, own_dv, sib_dv, dq_ref, q_head, g_head, turned):
    sides = ((own_k, own_v, own_dk, own_dv), (sib_k, sib_v, sib_dk, sib_dv))
    for p, (k_ref, v_ref, dk_ref, dv_ref) in enumerate(sides):

        def use(k_part, probs, dscore, p=p, dk_ref=dk_ref, dv_ref=dv_ref):
            key_terms(probs, dscore, q_head, g_head, dk_ref, dv_ref)
            query_terms(p, turned, k_part, dscore)

        scored(z_first, p, info, (k_ref, v_ref), q_ref, g_ref, st_ref, q_head, g_head, use)

    write_query_terms(info, turned, dq_ref)


def complete_kernel(half, info, *refs):
    sibs, (own_dk, own_dv, held, sems) = refs[:4], refs[-4:]
    span = half // PARTS
    loads, stores = [], []
    for n, sib in enumerate(sibs):
        part, own = n // 2, (own_dk, own_dv)[n % 2]
        at = pl.multiple_of((1 - info[0]) * half + part * span, span)
        loads.append(pltpu.make_async_copy(sib, held.at[n], sems.at[0, n]))
        stores.append(pltpu.make_async_copy(held.at[n], own.at[:, pl.ds(at, span)], sems.at[1, n]))
    for load in loads:
        load.start()
    for load, store in zip(loads, stores):
        load.wait()
        store.start()
    for store in stores:
        store.wait()


PARTS = 2


def blocks(slots, pairs, shape, part):
    span, steps = LANES, pairs
    first = part * (steps // PARTS)
    own = pl.BlockSpec((slots, span), lambda i, info: (0, info[0] * steps + first + i))
    sib = pl.BlockSpec((slots, span), lambda i, info: (0, first + i))
    q_block, g_block = (
        pl.BlockSpec(shape[:3] + (1, shape[4], span), lambda i, info, t=t: (0, 0, 0, t, 0, i))
        for t in range(2)
    )
    return own, [own, sib, own, sib, q_block, g_block], first, steps // PARTS


def sizes(operands):
    slots, half = operands[2].shape
    shape = operands[5].shape
    all_rows = shape[0] * shape[1] * shape[2] * shape[4]
    return slots, half, half // LANES, all_rows, all_rows // QRY


LIMIT = pltpu.CompilerParams(
    dimension_semantics=("arbitrary",), vmem_limit_bytes=58 * 1024 * 1024
)


def row_stats(operands, part, begun):
    slots, half, pairs, all_rows, rows = sizes(operands)
    own, in_blocks, first, steps = blocks(slots, pairs, operands[5].shape, part)
    return pl.pallas_call(
        functools.partial(stats_kernel, part == 0),
        grid_spec=pltpu.PrefetchScalarGridSpec(
            num_scalar_prefetch=1,
            grid=(steps,),
            in_specs=in_blocks + [pl.BlockSpec(memory_space=pl.ANY)] * len(begun),
            out_specs=pl.BlockSpec(
                (4, 2 * QRY, rows // 2), lambda i, info: (first + i, 0, 0)
            ),
            scratch_shapes=[pltpu.VMEM((2, rows, LANES), BF16)] * 2
            + [pltpu.VMEM((2, 2, 4, rows // 2), F32)],
        ),
        out_shape=jax.ShapeDtypeStruct((4 * pairs, 2 * QRY, rows // 2), F32),
        input_output_aliases={7: 0} if begun else {},
        compiler_params=LIMIT,
        cost_estimate=pl.CostEstimate(
            flops=4 * slots * rows * half, bytes_accessed=5 << 20,
            transcendentals=slots * rows * half // HDIM,
        ),
        name="row_stats",
    )(*operands, *begun)


def merge_stats(stats):
    return pl.pallas_call(
        merge_kernel,
        out_shape=jax.ShapeDtypeStruct(stats.shape, F32),
        in_specs=[pl.BlockSpec(memory_space=pltpu.VMEM)],
        out_specs=pl.BlockSpec(memory_space=pltpu.VMEM),
        name="merge_stats",
    )(stats)


def key_specs(operands, part):
    slots, half, pairs, all_rows, rows = sizes(operands)
    own = blocks(slots, pairs, operands[5].shape, part)[0]
    sib = pl.BlockSpec((slots, LANES), lambda i, info: (0, i))
    whole = jax.ShapeDtypeStruct((slots, 2 * half), BF16)
    half_part = jax.ShapeDtypeStruct((slots, half // PARTS), BF16)
    return [own, sib, own, sib], [whole, half_part, whole, half_part]


def query_specs(operands):
    slots, half, pairs, all_rows, rows = sizes(operands)
    spec = pl.BlockSpec((all_rows, LANES), lambda i, info: (0, i))
    scratch = pltpu.VMEM((2, LANES, rows), F32)
    return [spec], [jax.ShapeDtypeStruct((all_rows, half // PARTS), BF16)], [scratch]


def call(kernel, operands, stats, part, out_specs, out_shape, scratch, begun, share, name):
    slots, half, pairs, all_rows, rows = sizes(operands)
    own, in_blocks, first, steps = blocks(slots, pairs, operands[5].shape, part)
    stat = pl.BlockSpec((4, 2 * QRY, rows // 2), lambda i, info: (first + i, 0, 0))
    return pl.pallas_call(
        functools.partial(kernel, part == 0),
        grid_spec=pltpu.PrefetchScalarGridSpec(
            num_scalar_prefetch=1,
            grid=(steps,),
            in_specs=in_blocks + [stat] + [pl.BlockSpec(memory_space=pl.ANY)] * len(begun),
            out_specs=out_specs,
            scratch_shapes=[pltpu.VMEM((2, rows, LANES), BF16)] * 2 + scratch,
        ),
        out_shape=out_shape,
        input_output_aliases={8: 0, 9: 2} if begun else {},
        compiler_params=LIMIT,
        cost_estimate=pl.CostEstimate(
            flops=share * slots * rows * half, bytes_accessed=share << 20,
            transcendentals=slots * rows * half // HDIM,
        ),
        name=name,
    )(*operands, stats, *begun)


def query_gradients(operands, stats, part):
    specs, shapes, scratch = query_specs(operands)
    return call(
        dq_kernel, operands, stats, part, specs, shapes, scratch, [], 6, "query_gradients"
    )[0]


def key_gradients(operands, stats, part, begun):
    specs, shapes = key_specs(operands, part)
    return call(dkv_kernel, operands, stats, part, specs, shapes, [], begun, 8, "key_gradients")


def gradients(operands, stats, part):
    specs, shapes = key_specs(operands, part)
    more_specs, more_shapes, scratch = query_specs(operands)
    return call(
        grads_kernel, operands, stats, part, specs + more_specs, shapes + more_shapes, scratch,
        [], 10, "gradients",
    )


def completed(info, sibs, own_dk, own_dv):
    anywhere = pl.BlockSpec(memory_space=pl.ANY)
    shape = jax.ShapeDtypeStruct(own_dk.shape, BF16)
    return pl.pallas_call(
        functools.partial(complete_kernel, own_dk.shape[1] // 2),
        grid_spec=pltpu.PrefetchScalarGridSpec(
            num_scalar_prefetch=1,
            grid=(1,),
            in_specs=[anywhere] * 6,
            out_specs=[anywhere] * 2,
            scratch_shapes=[
                pltpu.VMEM((4,) + sibs[0].shape, BF16), pltpu.SemaphoreType.DMA((2, 4))
            ],
        ),
        out_shape=[shape, shape],
        input_output_aliases={5: 0, 6: 1},
        cost_estimate=pl.CostEstimate(flops=0, bytes_accessed=8 << 20, transcendentals=0),
        name="complete_keys",
    )(info, *sibs, own_dk, own_dv)


def per_device(x_size, z_size, queries, keys, values, grad_out, lengths, slot_query):
    chips = x_size * z_size
    core = lax.axis_index("core")
    width = keys.shape[2]
    half = width // 2
    span = half // PARTS
    keys, values = keys[0], values[0]

    mine = jnp.concatenate([slot_query, lengths])
    theirs = swap_cores(mine)
    info = jnp.stack([core, mine[0], theirs[0], mine[1], theirs[1]]).astype(jnp.int32)

    def features(value, at, count):
        return lax.dynamic_slice_in_dim(value, at, count, value.ndim - 1)

    both = lax.all_gather(jnp.stack([queries, grad_out]), "core", axis=0, tiled=False)
    own = [
        lax.dynamic_slice_in_dim(both, core * half + part * span, span, 3) for part in range(PARTS)
    ]
    gathered = (
        gather_x_then_z(own[0], x_size),
        gather_z_then_x(own[1], x_size, z_size),
    )
    sib_k = swap_cores(features(keys, (1 - core) * half, half))
    sib_v = swap_cores(features(values, (1 - core) * half, half))
    operands = [(info, keys, sib_k, values, sib_v, rows, rows) for rows in gathered]
    all_rows = sizes(operands[0])[3]

    stats = []
    for part in range(PARTS):
        stats = [row_stats(operands[part], part, stats)]
    stats = lax.all_to_all(stats[0], CHIP, 0, 0, tiled=True)
    stats = lax.all_to_all(merge_stats(stats), CHIP, 0, 0, tiled=True)

    held = all_rows // chips
    own_rows = held // 2

    def to_owners(dq):
        return lax.all_to_all(dq.reshape(chips, held, span), CHIP, 0, 0, tiled=True)

    first_terms = to_owners(query_gradients(operands[0], stats, 0))
    own_dk, sib_dk_1, own_dv, sib_dv_1, dq = gradients(operands[1], stats, 1)
    second_terms = to_owners(dq)
    sibs = [swap_cores(sib_dk_1), swap_cores(sib_dv_1)]
    stats, first_terms = lax.optimization_barrier((stats, first_terms))
    own_dk, sib_dk_0, own_dv, sib_dv_0 = key_gradients(operands[0], stats, 0, [own_dk, own_dv])
    sibs = [swap_cores(sib_dk_0), swap_cores(sib_dv_0)] + sibs
    own_dk, own_dv = completed(info, sibs, own_dk, own_dv)
    own_dk, second_terms = lax.optimization_barrier((own_dk, second_terms))
    sums = [
        jnp.sum(terms.astype(F32), axis=0).astype(BF16) for terms in (first_terms, second_terms)
    ]

    summed = jnp.concatenate(sums, axis=1)
    kept = lax.dynamic_slice_in_dim(summed, core * own_rows, own_rows, 0)
    given = swap_cores(lax.dynamic_slice_in_dim(summed, (1 - core) * own_rows, own_rows, 0))
    grad_queries = jnp.where(
        core == 0, jnp.concatenate([kept, given], 1), jnp.concatenate([given, kept], 1)
    )
    return grad_queries, own_dk[None], own_dv[None]


def solution(mesh):
    groups = mesh.devices.shape[0]
    x_size, z_size = 4, 8
    fine = Mesh(
        mesh.devices.reshape(groups, x_size, z_size, 2), ("group", "x", "z", "core")
    )
    at = ("group", "x", "z", "core")
    return jax.shard_map(
        functools.partial(per_device, x_size, z_size),
        mesh=fine,
        in_specs=(P(at, None), P(at, None, None), P(at, None, None), P(at, None), P(at), P(at)),
        out_specs=(P(at, None), P(at, None, None), P(at, None, None)),
        check_vma=False,
    )
```
